256 devices in a mesh: row: 16 (over y, x_hi, core), col: 16 (over x_lo, z).
Axes of the slice: x: 4 (x_hi: 2, x_lo: 2; x = x_hi * 2 + x_lo), y: 4, z: 8, core: 2. Of those that a mesh axis runs over, the one named last changes fastest.
Arguments:
- inputs: bfloat16 [512, 8192], P('col', 'row'), may hold values from -6 to 6
- out_grad: bfloat16 [512, 8192], P('col', 'row'), may hold values from -6 to 6
- gate_weight: bfloat16 [8192, 29568], P('row', 'col'), may hold values from -0.0625 to 0.0625
- up_weight: bfloat16 [8192, 29568], P('row', 'col'), may hold values from -0.0625 to 0.0625
- down_weight: bfloat16 [29568, 8192], P('col', 'row'), may hold values from -0.03125 to 0.03125
Outputs:
- grad_input: bfloat16 [512, 8192], P('col', 'row')
- grad_gate: bfloat16 [8192, 29568], P('row', 'col')
- grad_up: bfloat16 [8192, 29568], P('row', 'col')
- grad_down: bfloat16 [29568, 8192], P('col', 'row')
The draws below stay inside these ranges and needn't reach their ends.
All inputs are finite; a program needn't handle non-finite values.
Results may differ from the reference program's by a relative error of at most 0.0049.
Values may be sent and summed in bfloat16 or wider, within the bound.
A program may use at most 128 MiB of HBM per device.

```python
import jax
import jax.numpy as jnp

D = 8192
FF = 29568
TOKENS = 512


def steps_of(stream_key, dims, pieces, smallest, top_value):
    level, own = 1.0, jax.random.fold_in(stream_key, 6)
    for dim, parts in pieces:
        heights = jnp.exp(jax.random.uniform(jax.random.fold_in(own, dim), (parts,), jnp.float32, smallest / len(pieces), top_value / len(pieces)))
        level = level * jnp.repeat(heights, dims[dim] // parts).reshape([-1 if axis == dim else 1 for axis in range(len(dims))])
    return level


def scatter_about(rng, dims, width, limit, split=(), dtype=jnp.bfloat16):
    drawn = width * jax.random.normal(rng, dims, jnp.float32)
    if split:
        drawn = drawn * steps_of(rng, dims, split, -0.22, 0.18)
    return jnp.clip(drawn, -limit, limit).astype(dtype)


def setup_inputs(seed: int = 0) -> dict:
    arg_keys = jax.random.split(jax.random.key(seed), 6)
    inputs = scatter_about(arg_keys[0], (TOKENS, D), 1.0, 6.0, ((0, 16), (1, 16)))
    out_grad = scatter_about(arg_keys[1], (TOKENS, D), 1.0, 6.0, ((0, 16), (1, 16)))
    gate_weight = scatter_about(arg_keys[2], (D, FF), D ** -0.5, 0.0625, ((0, 16), (1, 16)))
    up_weight = scatter_about(arg_keys[3], (D, FF), D ** -0.5, 0.0625, ((0, 16), (1, 16)))
    down_weight = scatter_about(arg_keys[4], (FF, D), FF ** -0.5, 0.03125, ((0, 16), (1, 16)))
    return dict(inputs=inputs, out_grad=out_grad, gate_weight=gate_weight, up_weight=up_weight, down_weight=down_weight)


def reference(inputs, out_grad, gate_weight, up_weight, down_weight):
    gate = jnp.dot(inputs, gate_weight, preferred_element_type=jnp.float32)
    up = jnp.dot(inputs, up_weight, preferred_element_type=jnp.float32)
    back = jnp.dot(out_grad, down_weight.T, preferred_element_type=jnp.float32)
    sig = jax.nn.sigmoid(gate)
    act = gate * sig
    hidden = (act * up).astype(jnp.bfloat16)
    dgate = (back * up * sig * (1.0 + gate * (1.0 - sig))).astype(jnp.bfloat16)
    dup = (back * act).astype(jnp.bfloat16)
    grad_down = jnp.dot(hidden.T, out_grad, preferred_element_type=jnp.float32).astype(jnp.bfloat16)
    grad_gate = jnp.dot(inputs.T, dgate, preferred_element_type=jnp.float32).astype(jnp.bfloat16)
    grad_up = jnp.dot(inputs.T, dup, preferred_element_type=jnp.float32).astype(jnp.bfloat16)
    grad_input = (jnp.dot(dgate, gate_weight.T, preferred_element_type=jnp.float32)
                  + jnp.dot(dup, up_weight.T, preferred_element_type=jnp.float32)).astype(jnp.bfloat16)
    return grad_input, grad_gate, grad_up, grad_down
```

```python
import functools

import jax
import jax.numpy as jnp
from jax import lax
from jax.experimental import pallas as pl
from jax.experimental.pallas import tpu as pltpu
from jax.sharding import PartitionSpec as P

MESH = pl.DeviceIdType.MESH
F32, BF16 = jnp.float32, jnp.bfloat16

NEAR = [(dz, dx) for dz in (0, 1, -1, 2, -2, 3, -3, 4) for dx in (0, 1)]
OWNERS = [(dy, dh) for dy in (1, 3, 2, 0) for dh in (0, 1) if (dy, dh) != (0, 0)]
CHUNK = 640
UNITS = [(g, k) for g in range(2) for k in range(3)]


def contract(left, right, left_dim, right_dim):
    return lax.dot_general(
        left,
        right,
        (((left_dim,), (right_dim,)), ((), ())),
        preferred_element_type=F32,
    )


def pointwise(gate, up, back):
    sig = jax.nn.sigmoid(gate)
    act = gate * sig
    hidden = act * up
    dgate = back * up * sig * (1.0 + gate * (1.0 - sig))
    dup = back * act
    return hidden.astype(BF16), dgate.astype(BF16), dup.astype(BF16)


def kernel(
    x_in, g_in, wg_in, wu_in, wd_in,
    gi_out, gg_out, gu_out, gd_out,
    wg, wu, wd, x_all, g_all, x_t, part, pair, terms, got, acts, gi_acc, gi_send,
    gi_got, gg, gu, gd, gi,
    w_sem, gx_send, gx_recv, gg_send, gg_recv, pair_send, pair_recv, rs_send, rs_recv,
    ag_send, ag_recv, fw_send, fw_recv, gi_ssem, gi_rsem, out_sem,
):
    row, col = lax.axis_index("row"), lax.axis_index("col")
    y, h, c = row // 4, (row // 2) % 2, row % 2
    xl, z = col // 8, col % 8
    me = row // 2
    ff = wg.shape[1]

    def in_row(dy, dh):
        return ((y + dy) % 4) * 2 + (h + dh) % 2

    def owner_at(dy, dh):
        return {"row": in_row(dy, dh) * 2 + c, "col": col}

    def near_at(dz, dx):
        return {"row": row, "col": ((xl + dx) % 2) * 8 + (z + dz + 8) % 8}

    partner = {"row": me * 2 + 1 - c, "col": col}

    def remote(src, dst, send, recv, to):
        return pltpu.make_async_remote_copy(
            src_ref=src, dst_ref=dst, send_sem=send, recv_sem=recv, device_id=to, device_id_type=MESH
        )

    def width(k):
        return min(CHUNK, ff - k * CHUNK)

    loads = [
        pltpu.make_async_copy(src, dst, w_sem.at[i])
        for i, (src, dst) in enumerate(
            [(x_in, x_all.at[0]), (g_in, g_all.at[0]), (wg_in, wg), (wu_in, wu), (wd_in, wd)]
        )
    ]
    for load in loads:
        load.start()

    barrier = pltpu.get_barrier_semaphore()
    peers = [partner] + [owner_at(*s) for s in OWNERS] + [near_at(*s) for s in NEAR[1:]]
    for peer in peers:
        pl.semaphore_signal(barrier, inc=1, device_id=peer, device_id_type=MESH)
    pl.semaphore_wait(barrier, len(peers))

    gathers = {}
    for first in (0, 8):
        for name, src, dst, send, recv in (
            ("x", x_in, x_all, gx_send, gx_recv),
            ("g", g_in, g_all, gg_send, gg_recv),
        ):
            for i in range(max(first, 1), first + 8):
                dz, dx = NEAR[i]
                copy = remote(src, dst.at[i], send.at[i], recv.at[i], near_at(-dz, dx))
                copy.start()
                gathers[name, i] = copy

    started = list(gathers.values())

    def landed(name, group):
        for i in range(max(group * 8, 1), group * 8 + 8):
            gathers[name, i].wait_recv()
        if group == 0:
            loads[0 if name == "x" else 1].wait()

    def tokens(ref, group):
        return ref[group * 8 : group * 8 + 8].reshape(256, 512)

    pairs, scatters, spreads, forwards = {}, {}, {}, {}

    def multiply(u):
        g, k = UNITS[u]
        w = width(k)
        lanes = slice(k * CHUNK, k * CHUNK + w)
        if w < CHUNK:
            part[u, :, :, :, :, CHUNK - 128 :] = jnp.zeros((3, 2, 8, 16, 128), F32)
        if k == 0:
            landed("x", g)
        if u == 0:
            loads[2].wait()
            loads[3].wait()
        xs = tokens(x_all, g)
        part[u, 0, :, :, :, :w] = contract(xs, wg[:, lanes], 1, 0).reshape(2, 8, 16, w)
        part[u, 1, :, :, :, :w] = contract(xs, wu[:, lanes], 1, 0).reshape(2, 8, 16, w)
        if k == 0:
            landed("g", g)
        if u == 0:
            loads[4].wait()
        part[u, 2, :, :, :, :w] = contract(tokens(g_all, g), wd[lanes, :], 1, 1).reshape(2, 8, 16, w)
        pairs[u] = remote(part.at[u, :, 1 - c], pair.at[u], pair_send.at[u], pair_recv.at[u], partner)
        pairs[u].start()

    def scatter(u):
        pairs[u].wait_recv()
        for a in range(3):
            terms[u, a] = (part[u, a, c] + pair[u, a]).astype(BF16)
        for i, step in enumerate(OWNERS):
            copy = remote(
                terms.at[u, :, in_row(*step)], got.at[u, i], rs_send.at[u, i], rs_recv.at[u, i], owner_at(*step)
            )
            copy.start()
            scatters[u, i] = copy

    def reduce(u):
        for i in range(7):
            scatters[u, i].wait_recv()
        sums = []
        for a in range(3):
            total = part[u, a, c, me] + pair[u, a, me]
            for i in range(7):
                total = total + got[u, i, a].astype(F32)
            sums.append(total)
        for a, value in enumerate(pointwise(*sums)):
            acts[u, a, c, me] = value
        for i, step in enumerate(OWNERS):
            block = acts.at[u, :, c, me]
            copy = remote(block, block, ag_send.at[u, i], ag_recv.at[u, i], owner_at(*step))
            copy.start()
            spreads[u, i] = copy

    def forward(u):
        for i in range(7):
            spreads[u, i].wait_recv()
        half = acts.at[u, :, c]
        copy = remote(half, half, fw_send.at[u], fw_recv.at[u], partner)
        copy.start()
        forwards[u] = copy

    def act(u, a):
        return acts[u, a].reshape(256, CHUNK)[:, : width(UNITS[u][1])]

    gi_copies = {}

    def input_grad(u):
        g, k = UNITS[u]
        lanes = slice(k * CHUNK, k * CHUNK + width(k))
        forwards[u].wait_recv()
        term = contract(act(u, 1), wg[:, lanes], 1, 1) + contract(act(u, 2), wu[:, lanes], 1, 1)
        if k > 0:
            term = term + gi_acc[g]
        gi_acc[g] = term
        if k == 2:
            gi_send[g] = term.astype(BF16).reshape(8, 32, 512)
            for b in range(8):
                i = g * 8 + b
                if i:
                    copy = remote(gi_send.at[g, b], gi_got.at[i], gi_ssem.at[i], gi_rsem.at[i], near_at(*NEAR[i]))
                    copy.start()
                    gi_copies[i] = copy

    def weight_grads(k):
        w = width(k)
        lanes = slice(k * CHUNK, k * CHUNK + w)
        for a, out in ((1, gg), (2, gu)):
            total = contract(x_t[:, :256], act(k, a), 1, 0) + contract(x_t[:, 256:], act(k + 3, a), 1, 0)
            out[:, lanes] = total.astype(BF16)
        total = contract(act(k, 0), tokens(g_all, 0), 0, 0) + contract(act(k + 3, 0), tokens(g_all, 1), 0, 0)
        gd[lanes, :] = total.astype(BF16)

    for u in range(3):
        multiply(u)
        scatter(u)
    for u in range(3):
        reduce(u)
        multiply(u + 3)
        scatter(u + 3)
    x_t[...] = x_all[...].reshape(512, 512).T
    forward(0)
    reduce(3)
    forward(1)
    input_grad(0)
    reduce(4)
    forward(2)
    input_grad(1)
    reduce(5)
    input_grad(2)
    forward(3)
    input_grad(3)
    weight_grads(0)
    forward(4)
    input_grad(4)
    weight_grads(1)
    forward(5)
    input_grad(5)
    weight_grads(2)
    outs = [
        pltpu.make_async_copy(src, dst, out_sem.at[i])
        for i, (src, dst) in enumerate([(gg, gg_out), (gu, gu_out), (gd, gd_out), (gi, gi_out)])
    ]
    for out in outs[:3]:
        out.start()
    total = gi_acc[0, :32]
    for i in range(1, 16):
        gi_copies[i].wait_recv()
        total = total + gi_got[i].astype(F32)
    gi[...] = total.astype(BF16)
    outs[3].start()
    for group in (gathers, pairs, scatters, spreads, forwards, gi_copies):
        for copy in group.values():
            copy.wait_send()
    for out in outs:
        out.wait()


def on_device(inputs, out_grad, gate_weight, up_weight, down_weight):
    rows, depth = inputs.shape
    ff = gate_weight.shape[1]
    units = len(UNITS)
    dma = pltpu.SemaphoreType.DMA
    vmem = pltpu.VMEM
    flops = 9 * 2 * 512 * depth * ff
    moved = 2 * 6 * depth * ff
    return pl.pallas_call(
        kernel,
        out_shape=(
            jax.ShapeDtypeStruct(inputs.shape, BF16),
            jax.ShapeDtypeStruct(gate_weight.shape, BF16),
            jax.ShapeDtypeStruct(up_weight.shape, BF16),
            jax.ShapeDtypeStruct(down_weight.shape, BF16),
        ),
        in_specs=[pl.BlockSpec(memory_space=pl.ANY)] * 5,
        out_specs=[pl.BlockSpec(memory_space=pl.ANY)] * 4,
        scratch_shapes=[
            vmem(gate_weight.shape, BF16),
            vmem(up_weight.shape, BF16),
            vmem(down_weight.shape, BF16),
            vmem((16, rows, depth), BF16),
            vmem((16, rows, depth), BF16),
            vmem((depth, 512), BF16),
            vmem((units, 3, 2, 8, 16, CHUNK), F32),
            vmem((units, 3, 8, 16, CHUNK), F32),
            vmem((units, 3, 8, 16, CHUNK), BF16),
            vmem((units, 7, 3, 16, CHUNK), BF16),
            vmem((units, 3, 2, 8, 16, CHUNK), BF16),
            vmem((2, 256, depth), F32),
            vmem((2, 8, rows, depth), BF16),
            vmem((16, rows, depth), BF16),
            vmem(gate_weight.shape, BF16),
            vmem(up_weight.shape, BF16),
            vmem(down_weight.shape, BF16),
            vmem(inputs.shape, BF16),
            dma((5,)),
            dma((16,)),
            dma((16,)),
            dma((16,)),
            dma((16,)),
            dma((units,)),
            dma((units,)),
            dma((units, 7)),
            dma((units, 7)),
            dma((units, 7)),
            dma((units, 7)),
            dma((units,)),
            dma((units,)),
            dma((16,)),
            dma((16,)),
            dma((4,)),
        ],
        compiler_params=pltpu.CompilerParams(
            collective_id=0, has_side_effects=True, vmem_limit_bytes=62 << 20
        ),
        cost_estimate=pl.CostEstimate(flops=flops, bytes_accessed=moved, transcendentals=0),
    )(inputs, out_grad, gate_weight, up_weight, down_weight)


def solution(mesh):
    placed = (P("col", "row"), P("col", "row"), P("row", "col"), P("row", "col"), P("col", "row"))
    return jax.shard_map(
        on_device,
        mesh=mesh,
        in_specs=placed,
        out_specs=(P("col", "row"), P("row", "col"), P("row", "col"), P("col", "row")),
        check_vma=False,
    )
```

```python
import functools

import jax
import jax.numpy as jnp
from jax import lax
from jax.experimental import pallas as pl
from jax.experimental.pallas import tpu as pltpu
from jax.sharding import PartitionSpec as P

MESH = pl.DeviceIdType.MESH
F32, BF16 = jnp.float32, jnp.bfloat16

NEAR = [(0, 0), (0, 1), (1, 0), (1, 1), (-1, 0), (-1, 1), (2, 0), (-2, 0)]
NEAR += [(2, 1), (-2, 1), (3, 0), (3, 1), (-3, 0), (-3, 1), (4, 0), (4, 1)]
CHUNK = 640
UNITS = [(g, k) for g in range(2) for k in range(3)]
SUM_Y_FIRST = (False, True, False, False, False, True)
SPREAD_X_FIRST = (True, True, False, True, False, True)


def contract(left, right, left_dim, right_dim):
    return lax.dot_general(
        left,
        right,
        (((left_dim,), (right_dim,)), ((), ())),
        preferred_element_type=F32,
    )


def pointwise(gate, up, back):
    sig = jax.nn.sigmoid(gate)
    act = gate * sig
    hidden = act * up
    dgate = back * up * sig * (1.0 + gate * (1.0 - sig))
    dup = back * act
    return hidden.astype(BF16), dgate.astype(BF16), dup.astype(BF16)


def kernel(
    x_in, g_in, wg_in, wu_in, wd_in,
    gi_out, gg_out, gu_out, gd_out,
    wg, wu, wd, x_all, g_all, part, pair, terms, got, mid, cross, got_cross,
    acts, gi_acc, gi_send, gi_got, gg, gu, gd, gi,
    w_sem, near_send, near_recv, pair_send, pair_recv, sum_send, cross_send, sum_recv,
    act_send, act_recv, half_send, half_recv, gi_ssem, gi_rsem, out_sem,
):
    row, col = lax.axis_index("row"), lax.axis_index("col")
    y, h, c = row // 4, (row // 2) % 2, row % 2
    xl, z = col // 8, col % 8
    ff = wg.shape[0]

    def along(dy):
        return (y + dy) % 4

    def owner_at(dy, dh):
        return {"row": (along(dy) * 2 + (h + dh) % 2) * 2 + c, "col": col}

    def near_at(dz, dx):
        return {"row": row, "col": ((xl + dx) % 2) * 8 + (z + dz + 8) % 8}

    partner = {"row": row + 1 - 2 * c, "col": col}
    across = owner_at(0, 1)

    def remote(src, dst, send, recv, to):
        return pltpu.make_async_remote_copy(
            src_ref=src, dst_ref=dst, send_sem=send, recv_sem=recv, device_id=to, device_id_type=MESH
        )

    def settle(ref, sem):
        remote(ref, ref, sem, sem, partner).wait_recv()

    def width(k):
        return min(CHUNK, ff - k * CHUNK)

    loads = [
        pltpu.make_async_copy(src, dst, w_sem.at[i])
        for i, (src, dst) in enumerate(
            [(x_in, x_all.at[0]), (g_in, g_all.at[0]), (wg_in, wg), (wu_in, wu), (wd_in, wd)]
        )
    ]
    for load in loads:
        load.start()

    with jax.named_scope("greet"):
      barrier = pltpu.get_barrier_semaphore()
    peers = [partner, across] + [owner_at(dy, 0) for dy in (1, 2, 3)]
    peers += [near_at(0, 1), near_at(1, 0), near_at(-1, 0)]
    for peer in peers:
        pl.semaphore_signal(barrier, inc=1, device_id=peer, device_id_type=MESH)
    pl.semaphore_wait(barrier, len(peers))

    def hand(n, slot, to, at):
        ref = (x_all, g_all)[n]
        src = (x_in, g_in)[n] if slot == 0 else ref.at[slot]
        remote(src, ref.at[at], near_send.at[n], near_recv.at[n, at], to).start()

    seen = set()

    def arrived(n, slot):
        ref = (x_all, g_all)[n]
        if (n, slot) not in seen:
            seen.add((n, slot))
            if slot:
                remote(ref.at[slot], ref.at[slot], near_send.at[n], near_recv.at[n, slot], partner).wait_recv()
            else:
                loads[n].wait()

    def slot_of(dz, dx):
        return NEAR.index((dz, dx))

    def gather(step, n):
        if step == 0:
            hand(n, 0, near_at(0, 1), slot_of(0, 1))
        dx = step % 2
        far = step // 2
        for way in (1, -1):
            if far == 3 and (way == 1) == bool(dx):
                continue
            slot = slot_of(-way * far, dx)
            if slot:
                arrived(n, slot)
        for way in (1, -1):
            if far == 3 and (way == 1) == bool(dx):
                continue
            to = -way * (far + 1) if far < 3 else 4
            hand(n, slot_of(-way * far, dx), near_at(way, 0), slot_of(to, dx))

    def landed(n, group):
        for slot in range(group * 8, group * 8 + 8):
            arrived(n, slot)

    def tokens(ref, group):
        return ref[group * 8 : group * 8 + 8].reshape(256, 512)

    def multiply(u, a, ref, weight):
        g, k = UNITS[u]
        w = width(k)
        if w < CHUNK:
            part[u, a, :, :, :, :, CHUNK - 128 :] = jnp.zeros((2, 2, 4, 16, 128), F32)
        product = contract(tokens(ref, g), weight[k * CHUNK : k * CHUNK + w, :], 1, 1)
        part[u, a, :, :, :, :, :w] = product.reshape(2, 2, 4, 16, w)
        remote(part.at[u, a, 1 - c], pair.at[u, a], pair_send.at[0], pair_recv.at[u], partner).start()

    def gate_up(u):
        g, k = UNITS[u]
        if k == 0:
            landed(0, g)
        if u == 0:
            loads[2].wait()
        multiply(u, 0, x_all, wg)
        if u == 0:
            loads[3].wait()
        multiply(u, 1, x_all, wu)

    def back(u):
        g, k = UNITS[u]
        if k == 0:
            landed(1, g)
        if u == 0:
            loads[4].wait()
        multiply(u, 2, g_all, wd)

    def sum_first(u):
        settle(pair.at[u], pair_recv.at[u])
        for a in range(3):
            if SUM_Y_FIRST[u]:
                terms[u, :, :, a] = (part[u, a, c] + pair[u, a]).astype(BF16)
            else:
                terms[u, 1 - h, :, a] = (part[u, a, c, 1 - h] + pair[u, a, 1 - h]).astype(BF16)
        if SUM_Y_FIRST[u]:
            for dy in (2, 1, 3):
                remote(
                    terms.at[u, :, along(dy)], got.at[u, 2 * dy - 2 : 2 * dy],
                    sum_send.at[u], sum_recv.at[u, 0], owner_at(dy, 0),
                ).start()
        else:
            remote(terms.at[u, 1 - h], got.at[u, :4], sum_send.at[u], sum_recv.at[u, 0], across).start()

    def sum_second(u):
        if SUM_Y_FIRST[u]:
            settle(got.at[u, :6], sum_recv.at[u, 0])
            n = sum(SUM_Y_FIRST[:u])
            for a in range(3):
                total = part[u, a, c, 1 - h, y] + pair[u, a, 1 - h, y]
                for i in range(3):
                    total = total + got[u, 2 * i + 1 - h, a].astype(F32)
                cross[n, a] = total
            remote(cross.at[n], got_cross.at[n], cross_send.at[0], sum_recv.at[u, 1], across).start()
        else:
            settle(got.at[u, :4], sum_recv.at[u, 0])
            for a in range(3):
                total = part[u, a, c, h] + pair[u, a, h] + got[u, :4, a].astype(F32)
                mid[u, :, a] = total.astype(BF16)
            for dy in (2, 1, 3):
                remote(
                    mid.at[u, along(dy)], got.at[u, 3 + dy], sum_send.at[u], sum_recv.at[u, 1], owner_at(dy, 0)
                ).start()

    def block(u, dy, dh, arrays=slice(0, 3)):
        return acts.at[u, arrays, c, (h + dh) % 2, along(dy)]

    def spread(u, sem, ref, to):
        remote(ref, ref, act_send.at[u], act_recv.at[u, sem], to).start()

    def reduce(u):
        totals = []
        n = sum(SUM_Y_FIRST[:u])
        if SUM_Y_FIRST[u]:
            settle(got_cross.at[n], sum_recv.at[u, 1])
        else:
            settle(got.at[u, 4:7], sum_recv.at[u, 1])
        for a in range(3):
            total = part[u, a, c, h, y] + pair[u, a, h, y]
            if SUM_Y_FIRST[u]:
                for i in range(3):
                    total = total + got[u, 2 * i + h, a].astype(F32)
                total = total + got_cross[n, a]
            else:
                total = total + got[u, y, a].astype(F32)
                for i in range(3):
                    total = total + got[u, 4 + i, a].astype(F32)
            totals.append(total)
        for a, value in enumerate(pointwise(*totals)):
            acts[u, a, c, h, y] = value
        own = block(u, 0, 0)
        if SPREAD_X_FIRST[u]:
            spread(u, 0, own, across)
            spread(u, 1, own, owner_at(1, 0))
            spread(u, 3, own, owner_at(3, 0))
        else:
            spread(u, 0, own, owner_at(1, 0))
            spread(u, 1, own, owner_at(3, 0))
            spread(u, 3, own, across)

    def spread_a(u):
        settle(block(u, 0, 0), act_recv.at[u, 0])
        if SPREAD_X_FIRST[u]:
            spread(u, 3, block(u, 0, 1), owner_at(1, 0))
            spread(u, 2, block(u, 0, 1), owner_at(3, 0))
        else:
            spread(u, 2, block(u, 3, 0, slice(0, 2)), owner_at(1, 0))
            spread(u, 3, block(u, 3, 0), across)

    def spread_b(u):
        settle(block(u, 0, 0), act_recv.at[u, 1])
        if SPREAD_X_FIRST[u]:
            spread(u, 3, block(u, 3, 0), owner_at(1, 0))
        else:
            spread(u, 2, block(u, 1, 0, slice(2, 3)), owner_at(3, 0))
            spread(u, 3, block(u, 1, 0), across)

    def spread_c(u):
        settle(block(u, 0, 0), act_recv.at[u, 2])
        if SPREAD_X_FIRST[u]:
            spread(u, 3, block(u, 1, 1), owner_at(3, 0))
        else:
            spread(u, 3, block(u, 2, 0), across)

    def spread_last(u):
        settle(got.at[u, :4], act_recv.at[u, 3])
        half = acts.at[u, :, c]
        remote(half, half, half_send.at[0], half_recv.at[u], partner).start()

    def act(u, a):
        return acts[u, a].reshape(256, CHUNK)[:, : width(UNITS[u][1])]

    def input_grad(u):
        g, k = UNITS[u]
        rows = slice(k * CHUNK, k * CHUNK + width(k))
        settle(acts.at[u, :, 1 - c], half_recv.at[u])
        term = contract(act(u, 1), wg[rows, :], 1, 0) + contract(act(u, 2), wu[rows, :], 1, 0)
        if k > 0:
            term = term + gi_acc[g]
        gi_acc[g] = term
        if k == 2:
            gi_send[g] = term.astype(BF16).reshape(8, 32, 512)
            for b in reversed(range(8)):
                i = g * 8 + b
                if i:
                    remote(gi_send.at[g, b], gi_got.at[i], gi_ssem.at[0], gi_rsem.at[0], near_at(*NEAR[i])).start()

    def weight_grads(k):
        rows = slice(k * CHUNK, k * CHUNK + width(k))
        for a, ref, out in ((1, x_all, gg), (2, x_all, gu), (0, g_all, gd)):
            total = contract(act(k, a), tokens(ref, 0), 0, 0) + contract(act(k + 3, a), tokens(ref, 1), 0, 0)
            out[rows, :] = total.astype(BF16)

    plan = [
        (gather, 0, 0), (gather, 0, 1), (gather, 1, 0), (gather, 1, 1),
        (gather, 2, 0), (gather, 2, 1), (gather, 3, 0), (gather, 3, 1),
        (gate_up, 0), (gate_up, 1), (gather, 4, 0), (gather, 4, 1),
        (back, 0), (back, 1), (gather, 5, 0), (gather, 5, 1),
        (gate_up, 2), (back, 2), (gather, 6, 0), (gather, 6, 1),
        (sum_first, 0), (gather, 7, 0), (gather, 7, 1), (sum_first, 1),
        (sum_first, 2), (gate_up, 3), (gate_up, 4), (back, 3),
        (back, 4), (gate_up, 5), (back, 5), (sum_first, 3),
        (sum_second, 0), (sum_second, 1), (sum_first, 4), (sum_first, 5),
        (reduce, 0), (sum_second, 2), (sum_second, 3), (reduce, 1),
        (reduce, 2), (reduce, 3), (sum_second, 4), (sum_second, 5),
        (spread_a, 0), (spread_b, 0), (spread_a, 1), (spread_b, 1),
        (spread_a, 2), (spread_b, 2), (reduce, 4), (spread_a, 3),
        (spread_b, 3), (spread_c, 0), (reduce, 5), (spread_c, 1),
        (spread_c, 2), (spread_a, 4), (spread_b, 4), (spread_c, 3),
        (spread_a, 5), (spread_last, 0), (spread_b, 5), (input_grad, 0),
        (spread_last, 1), (spread_last, 2), (spread_c, 4), (spread_last, 3),
        (input_grad, 1), (spread_c, 5), (input_grad, 2), (input_grad, 3),
        (spread_last, 4), (weight_grads, 0), (spread_last, 5), (input_grad, 4),
        (weight_grads, 1), (input_grad, 5), (weight_grads, 2),
    ]
    for stage, *at in plan:
        stage(*at)
    outs = [
        pltpu.make_async_copy(src, dst, out_sem.at[i])
        for i, (src, dst) in enumerate([(gg, gg_out), (gu, gu_out), (gd, gd_out), (gi, gi_out)])
    ]
    for out in outs[:3]:
        out.start()
    settle(gi_got.at[1:16], gi_rsem.at[0])
    total = gi_acc[0, :32]
    for i in range(1, 16):
        total = total + gi_got[i].astype(F32)
    gi[...] = total.astype(BF16)
    outs[3].start()
    settle(x_all.at[1:16], near_send.at[0])
    settle(g_all.at[1:16], near_send.at[1])
    settle(pair, pair_send.at[0])
    for u in range(len(UNITS)):
        settle(got.at[u, : 6 if SUM_Y_FIRST[u] else 7], sum_send.at[u])
        settle(got.at[u], act_send.at[u])
    settle(cross, cross_send.at[0])
    settle(terms, half_send.at[0])
    settle(gi_got.at[1:16], gi_ssem.at[0])
    for out in outs:
        out.wait()


def place(*refs):
    count = (len(refs) - 2) // 3
    sources, results, held = refs[:count], refs[count : 2 * count], refs[2 * count : 3 * count]
    ins = [pltpu.make_async_copy(a, b, refs[-2].at[i]) for i, (a, b) in enumerate(zip(sources, held))]
    outs = [pltpu.make_async_copy(a, b, refs[-1].at[i]) for i, (a, b) in enumerate(zip(held, results))]
    for copy in ins:
        copy.start()
    for taken, given in zip(ins, outs):
        taken.wait()
        given.start()
    for copy in outs:
        copy.wait()


def on_device(inputs, out_grad, gate_weight, up_weight, down_weight):
    rows, depth = inputs.shape
    gate_weight, up_weight = gate_weight.T, up_weight.T
    ff = gate_weight.shape[0]
    units = len(UNITS)
    dma = pltpu.SemaphoreType.DMA
    vmem = pltpu.VMEM
    weight = jax.ShapeDtypeStruct((ff, depth), BF16)
    results = (jax.ShapeDtypeStruct(inputs.shape, BF16), weight, weight, weight)
    anywhere = pl.BlockSpec(memory_space=pl.ANY)
    made = pl.pallas_call(
        kernel,
        out_shape=results,
        in_specs=[anywhere] * 5,
        out_specs=[anywhere] * 4,
        scratch_shapes=[
            vmem((ff, depth), BF16),
            vmem((ff, depth), BF16),
            vmem((ff, depth), BF16),
            vmem((16, rows, depth), BF16),
            vmem((16, rows, depth), BF16),
            vmem((units, 3, 2, 2, 4, 16, CHUNK), F32),
            vmem((units, 3, 2, 4, 16, CHUNK), F32),
            vmem((units, 2, 4, 3, 16, CHUNK), BF16),
            vmem((units, 7, 3, 16, CHUNK), BF16),
            vmem((units, 4, 3, 16, CHUNK), BF16),
            vmem((sum(SUM_Y_FIRST), 3, 16, CHUNK), F32),
            vmem((sum(SUM_Y_FIRST), 3, 16, CHUNK), F32),
            vmem((units, 3, 2, 2, 4, 16, CHUNK), BF16),
            vmem((2, 256, depth), F32),
            vmem((2, 8, rows, depth), BF16),
            vmem((16, rows, depth), BF16),
            vmem((ff, depth), BF16),
            vmem((ff, depth), BF16),
            vmem((ff, depth), BF16),
            vmem(inputs.shape, BF16),
            dma((5,)),
            dma((2,)),
            dma((2, 16)),
            dma((1,)),
            dma((units,)),
            dma((units,)),
            dma((1,)),
            dma((units, 2)),
            dma((units,)),
            dma((units, 4)),
            dma((1,)),
            dma((units,)),
            dma((1,)),
            dma((1,)),
            dma((4,)),
        ],
        compiler_params=pltpu.CompilerParams(
            collective_id=0, has_side_effects=True, vmem_limit_bytes=62 << 20
        ),
        cost_estimate=pl.CostEstimate(
            flops=18 * 512 * depth * ff, bytes_accessed=12 * depth * ff, transcendentals=0
        ),
    )(inputs, out_grad, gate_weight, up_weight, down_weight)
    grad_input, grad_gate, grad_up, grad_down = pl.pallas_call(
        place,
        out_shape=results,
        in_specs=[anywhere] * 4,
        out_specs=[anywhere] * 4,
        scratch_shapes=[vmem(a.shape, a.dtype) for a in results] + [dma((4,)), dma((4,))],
        compiler_params=pltpu.CompilerParams(vmem_limit_bytes=60 << 20),
    )(*made)
    return grad_input, grad_gate.T, grad_up.T, grad_down


def solution(mesh):
    placed = (P("col", "row"), P("col", "row"), P("row", "col"), P("row", "col"), P("col", "row"))
    return jax.shard_map(
        on_device,
        mesh=mesh,
        in_specs=placed,
        out_specs=(P("col", "row"), P("row", "col"), P("row", "col"), P("col", "row")),
        check_vma=False,
    )
```

```python
import functools

import jax
import jax.numpy as jnp
from jax import lax
from jax.experimental import pallas as pl
from jax.experimental.pallas import tpu as pltpu
from jax.sharding import PartitionSpec as P

MESH = pl.DeviceIdType.MESH
F32, BF16 = jnp.float32, jnp.bfloat16

NEAR = [(0, 0), (0, 1), (1, 0), (1, 1), (-1, 0), (-1, 1), (2, 0), (-2, 0)]
NEAR += [(2, 1), (-2, 1), (3, 0), (3, 1), (-3, 0), (-3, 1), (4, 0), (4, 1)]
CHUNK = 640
UNITS = [(g, k) for g in range(2) for k in range(3)]
SUM_Y_FIRST = (True, False, True, False, False, True)
SPREAD_X_FIRST = (True, True, False, False, True, True)


def contract(left, right, left_dim, right_dim):
    return lax.dot_general(
        left,
        right,
        (((left_dim,), (right_dim,)), ((), ())),
        preferred_element_type=F32,
    )


def pointwise(gate, up, back):
    sig = jax.nn.sigmoid(gate)
    act = gate * sig
    hidden = act * up
    dgate = back * up * sig * (1.0 + gate * (1.0 - sig))
    dup = back * act
    return hidden.astype(BF16), dgate.astype(BF16), dup.astype(BF16)


def kernel(
    x_in, g_in, wg_in, wu_in, wd_in,
    gi_out, gg_out, gu_out, gd_out,
    wg, wu, wd, x_all, g_all, part, pair, terms, got, mid, cross, got_cross,
    acts, gi_acc, gi_send, gi_got, gg, gu, gd, gi,
    w_sem, near_send, near_recv, pair_send, pair_recv, sum_send, cross_send, sum_recv,
    act_send, act_recv, half_send, half_recv, gi_ssem, gi_rsem, out_sem,
):
    row, col = lax.axis_index("row"), lax.axis_index("col")
    y, h, c = row // 4, (row // 2) % 2, row % 2
    xl, z = col // 8, col % 8
    ff = wg.shape[0]

    def along(dy):
        return (y + dy) % 4

    def owner_at(dy, dh):
        return {"row": (along(dy) * 2 + (h + dh) % 2) * 2 + c, "col": col}

    def near_at(dz, dx):
        return {"row": row, "col": ((xl + dx) % 2) * 8 + (z + dz + 8) % 8}

    partner = {"row": row + 1 - 2 * c, "col": col}
    across = owner_at(0, 1)

    def remote(src, dst, send, recv, to):
        return pltpu.make_async_remote_copy(
            src_ref=src, dst_ref=dst, send_sem=send, recv_sem=recv, device_id=to, device_id_type=MESH
        )

    def settle(ref, sem):
        remote(ref, ref, sem, sem, partner).wait_recv()

    def width(k):
        return min(CHUNK, ff - k * CHUNK)

    loads = [
        pltpu.make_async_copy(src, dst, w_sem.at[i])
        for i, (src, dst) in enumerate(
            [(x_in, x_all.at[0]), (g_in, g_all.at[0]), (wg_in, wg), (wu_in, wu), (wd_in, wd)]
        )
    ]
    for load in loads:
        load.start()

    with jax.named_scope("greet"):
      barrier = pltpu.get_barrier_semaphore()
    peers = [partner, across] + [owner_at(dy, 0) for dy in (1, 2, 3)]
    peers += [near_at(*step) for step in NEAR[1:8]]
    for peer in peers:
        pl.semaphore_signal(barrier, inc=1, device_id=peer, device_id_type=MESH)
    pl.semaphore_wait(barrier, len(peers))

    def hand(n, slot, to, at):
        ref = (x_all, g_all)[n]
        remote(ref.at[slot], ref.at[at], near_send.at[n], near_recv.at[n, at], to).start()

    seen = set()

    def arrived(n, slot):
        ref = (x_all, g_all)[n]
        if (n, slot) not in seen:
            seen.add((n, slot))
            if slot:
                remote(ref.at[slot], ref.at[slot], near_send.at[n], near_recv.at[n, slot], partner).wait_recv()
            else:
                loads[n].wait()

    def slot_of(dz, dx):
        return NEAR.index((dz, dx))

    def gather_near(n):
        arrived(n, 0)
        for slot in (6, 7, 3, 5, 2, 4, 1):
            dz, dx = NEAR[slot]
            hand(n, 0, near_at(-dz, dx), slot)

    def gather(far, dx, n):
        for way in (1, -1):
            if far == 3 and (way == 1) == bool(dx):
                continue
            slot = slot_of(-way * far, dx)
            arrived(n, slot)
            hand(n, slot, near_at(way, 0), slot_of(-way * (far + 1) if far < 3 else 4, dx))

    loaded = set()

    def weights_in(n):
        if n not in loaded:
            loaded.add(n)
            loads[n].wait()

    def landed(n, group):
        for slot in range(group * 8, group * 8 + 8):
            arrived(n, slot)

    def tokens(ref, group):
        return ref[group * 8 : group * 8 + 8].reshape(256, 512)

    def multiply(u, a, ref, weight):
        g, k = UNITS[u]
        w = width(k)
        if w < CHUNK:
            part[u, a, :, :, :, :, CHUNK - 128 :] = jnp.zeros((2, 2, 4, 16, 128), F32)
        product = contract(tokens(ref, g), weight[k * CHUNK : k * CHUNK + w, :], 1, 1)
        part[u, a, :, :, :, :, :w] = product.reshape(2, 2, 4, 16, w)
        remote(part.at[u, a, 1 - c], pair.at[u, a], pair_send.at[0], pair_recv.at[u], partner).start()

    def gate_up(u):
        landed(0, UNITS[u][0])
        weights_in(2)
        multiply(u, 0, x_all, wg)
        weights_in(3)
        multiply(u, 1, x_all, wu)

    def back(u):
        landed(1, UNITS[u][0])
        weights_in(4)
        multiply(u, 2, g_all, wd)

    def sum_first(u):
        settle(pair.at[u], pair_recv.at[u])
        for a in range(3):
            if SUM_Y_FIRST[u]:
                terms[u, :, :, a] = (part[u, a, c] + pair[u, a]).astype(BF16)
            else:
                terms[u, 1 - h, :, a] = (part[u, a, c, 1 - h] + pair[u, a, 1 - h]).astype(BF16)
        if SUM_Y_FIRST[u]:
            for dy in (2, 1, 3):
                remote(
                    terms.at[u, :, along(dy)], got.at[u, 2 * dy - 2 : 2 * dy],
                    sum_send.at[u], sum_recv.at[u, 0], owner_at(dy, 0),
                ).start()
        else:
            remote(terms.at[u, 1 - h], got.at[u, :4], sum_send.at[u], sum_recv.at[u, 0], across).start()

    def sum_second(u):
        if SUM_Y_FIRST[u]:
            settle(got.at[u, :6], sum_recv.at[u, 0])
            n = sum(SUM_Y_FIRST[:u])
            for a in range(3):
                total = part[u, a, c, 1 - h, y] + pair[u, a, 1 - h, y]
                for i in range(3):
                    total = total + got[u, 2 * i + 1 - h, a].astype(F32)
                cross[n, a] = total
            remote(cross.at[n], got_cross.at[n], cross_send.at[0], sum_recv.at[u, 1], across).start()
        else:
            settle(got.at[u, :4], sum_recv.at[u, 0])
            for a in range(3):
                total = part[u, a, c, h] + pair[u, a, h] + got[u, :4, a].astype(F32)
                mid[u, :, a] = total.astype(BF16)
            for dy in (2, 1, 3):
                remote(
                    mid.at[u, along(dy)], got.at[u, 3 + dy], sum_send.at[u], sum_recv.at[u, 1], owner_at(dy, 0)
                ).start()

    def block(u, dy, dh, arrays=slice(0, 3)):
        return acts.at[u, arrays, c, (h + dh) % 2, along(dy)]

    def spread(u, sem, ref, to):
        remote(ref, ref, act_send.at[u], act_recv.at[u, sem], to).start()

    def reduce(u):
        totals = []
        n = sum(SUM_Y_FIRST[:u])
        if SUM_Y_FIRST[u]:
            settle(got_cross.at[n], sum_recv.at[u, 1])
        else:
            settle(got.at[u, 4:7], sum_recv.at[u, 1])
        for a in range(3):
            total = part[u, a, c, h, y] + pair[u, a, h, y]
            if SUM_Y_FIRST[u]:
                for i in range(3):
                    total = total + got[u, 2 * i + h, a].astype(F32)
                total = total + got_cross[n, a]
            else:
                total = total + got[u, y, a].astype(F32)
                for i in range(3):
                    total = total + got[u, 4 + i, a].astype(F32)
            totals.append(total)
        for a, value in enumerate(pointwise(*totals)):
            acts[u, a, c, h, y] = value
        own = block(u, 0, 0)
        if SPREAD_X_FIRST[u]:
            spread(u, 0, own, across)
            spread(u, 1, own, owner_at(1, 0))
            spread(u, 3, own, owner_at(3, 0))
        else:
            spread(u, 0, own, owner_at(1, 0))
            spread(u, 1, own, owner_at(3, 0))
            spread(u, 3, own, across)

    def spread_a(u):
        settle(block(u, 0, 0), act_recv.at[u, 0])
        if SPREAD_X_FIRST[u]:
            spread(u, 3, block(u, 0, 1), owner_at(1, 0))
            spread(u, 2, block(u, 0, 1), owner_at(3, 0))
        else:
            spread(u, 2, block(u, 3, 0, slice(0, 2)), owner_at(1, 0))
            spread(u, 3, block(u, 3, 0), across)

    def spread_b(u):
        settle(block(u, 0, 0), act_recv.at[u, 1])
        if SPREAD_X_FIRST[u]:
            spread(u, 3, block(u, 3, 0), owner_at(1, 0))
        else:
            spread(u, 2, block(u, 1, 0, slice(2, 3)), owner_at(3, 0))
            spread(u, 3, block(u, 1, 0), across)

    def spread_c(u):
        settle(block(u, 0, 0), act_recv.at[u, 2])
        if SPREAD_X_FIRST[u]:
            spread(u, 3, block(u, 1, 1), owner_at(3, 0))
        else:
            spread(u, 3, block(u, 2, 0), across)

    def spread_last(u):
        settle(got.at[u, :4], act_recv.at[u, 3])
        half = acts.at[u, :, c]
        remote(half, half, half_send.at[0], half_recv.at[u], partner).start()

    def act(u, a):
        return acts[u, a].reshape(256, CHUNK)[:, : width(UNITS[u][1])]

    summed = [0, 0]

    def input_grad(u):
        g, k = UNITS[u]
        rows = slice(k * CHUNK, k * CHUNK + width(k))
        settle(acts.at[u, :, 1 - c], half_recv.at[u])
        term = contract(act(u, 1), wg[rows, :], 1, 0) + contract(act(u, 2), wu[rows, :], 1, 0)
        if summed[g] > 0:
            term = term + gi_acc[g]
        gi_acc[g] = term
        summed[g] += 1
        if summed[g] == 3:
            gi_send[g] = term.astype(BF16).reshape(8, 32, 512)
            for b in reversed(range(8)):
                i = g * 8 + b
                if i:
                    remote(gi_send.at[g, b], gi_got.at[i], gi_ssem.at[0], gi_rsem.at[0], near_at(*NEAR[i])).start()

    def weight_grads(k):
        rows = slice(k * CHUNK, k * CHUNK + width(k))
        for a, ref, out in ((1, x_all, gg), (2, x_all, gu), (0, g_all, gd)):
            total = contract(act(k, a), tokens(ref, 0), 0, 0) + contract(act(k + 3, a), tokens(ref, 1), 0, 0)
            out[rows, :] = total.astype(BF16)

    plan = [
        (gather_near, 0), (gather_near, 1),
        (gather, 1, 1, 0), (gate_up, 0), (gather, 2, 0, 0), (gate_up, 1),
        (gather, 1, 1, 1), (back, 0), (gather, 2, 0, 1), (back, 1),
        (gather, 2, 1, 0), (gather, 3, 0, 0), (gate_up, 2), (back, 2),
        (gather, 2, 1, 1), (gather, 3, 0, 1), (sum_first, 0), (sum_first, 1),
        (gather, 3, 1, 0), (gather, 3, 1, 1), (sum_first, 2), (gate_up, 3),
        (gate_up, 5), (gate_up, 4), (sum_second, 0), (back, 3),
        (back, 5), (sum_second, 1), (back, 4), (sum_first, 3),
        (sum_first, 5), (sum_first, 4), (sum_second, 2), (reduce, 0),
        (reduce, 1), (sum_second, 3), (sum_second, 5), (sum_second, 4),
        (reduce, 2), (reduce, 3), (spread_a, 0), (spread_b, 0),
        (spread_a, 1), (spread_b, 1), (reduce, 4), (spread_a, 2),
        (spread_b, 2), (reduce, 5), (spread_a, 3), (spread_b, 3),
        (spread_c, 0), (spread_c, 1), (spread_a, 4), (spread_b, 4),
        (spread_c, 2), (spread_c, 3), (spread_a, 5), (spread_b, 5),
        (spread_last, 0), (spread_last, 1), (input_grad, 0), (spread_c, 4),
        (input_grad, 1), (spread_last, 2), (spread_c, 5), (spread_last, 3),
        (input_grad, 2), (spread_last, 4), (input_grad, 3), (spread_last, 5),
        (weight_grads, 0), (input_grad, 4), (input_grad, 5), (weight_grads, 2),
        (weight_grads, 1),
    ]
    for stage, *at in plan:
        stage(*at)
    outs = [
        pltpu.make_async_copy(src, dst, out_sem.at[i])
        for i, (src, dst) in enumerate([(gg, gg_out), (gu, gu_out), (gd, gd_out), (gi, gi_out)])
    ]
    for out in outs[:3]:
        out.start()
    settle(gi_got.at[1:16], gi_rsem.at[0])
    total = gi_acc[0, :32]
    for i in range(1, 16):
        total = total + gi_got[i].astype(F32)
    gi[...] = total.astype(BF16)
    outs[3].start()
    settle(x_all.at[1:16], near_send.at[0])
    settle(g_all.at[1:16], near_send.at[1])
    settle(pair, pair_send.at[0])
    for u in range(len(UNITS)):
        settle(got.at[u, : 6 if SUM_Y_FIRST[u] else 7], sum_send.at[u])
        settle(got.at[u], act_send.at[u])
    settle(cross, cross_send.at[0])
    settle(terms, half_send.at[0])
    settle(gi_got.at[1:16], gi_ssem.at[0])
    for out in outs:
        out.wait()


def place(*refs):
    for source, result in zip(refs[:4], refs[4:]):
        result[...] = source[...]


def on_device(inputs, out_grad, gate_weight, up_weight, down_weight):
    rows, depth = inputs.shape
    gate_weight, up_weight = gate_weight.T, up_weight.T
    ff = gate_weight.shape[0]
    units = len(UNITS)
    dma = pltpu.SemaphoreType.DMA
    vmem = pltpu.VMEM
    weight = jax.ShapeDtypeStruct((ff, depth), BF16)
    results = (jax.ShapeDtypeStruct(inputs.shape, BF16), weight, weight, weight)
    anywhere = pl.BlockSpec(memory_space=pl.ANY)
    made = pl.pallas_call(
        kernel,
        out_shape=results,
        in_specs=[anywhere] * 5,
        out_specs=[anywhere] * 4,
        scratch_shapes=[
            vmem((ff, depth), BF16),
            vmem((ff, depth), BF16),
            vmem((ff, depth), BF16),
            vmem((16, rows, depth), BF16),
            vmem((16, rows, depth), BF16),
            vmem((units, 3, 2, 2, 4, 16, CHUNK), F32),
            vmem((units, 3, 2, 4, 16, CHUNK), F32),
            vmem((units, 2, 4, 3, 16, CHUNK), BF16),
            vmem((units, 7, 3, 16, CHUNK), BF16),
            vmem((units, 4, 3, 16, CHUNK), BF16),
            vmem((sum(SUM_Y_FIRST), 3, 16, CHUNK), F32),
            vmem((sum(SUM_Y_FIRST), 3, 16, CHUNK), F32),
            vmem((units, 3, 2, 2, 4, 16, CHUNK), BF16),
            vmem((2, 256, depth), F32),
            vmem((2, 8, rows, depth), BF16),
            vmem((16, rows, depth), BF16),
            vmem((ff, depth), BF16),
            vmem((ff, depth), BF16),
            vmem((ff, depth), BF16),
            vmem(inputs.shape, BF16),
            dma((5,)),
            dma((2,)),
            dma((2, 16)),
            dma((1,)),
            dma((units,)),
            dma((units,)),
            dma((1,)),
            dma((units, 2)),
            dma((units,)),
            dma((units, 4)),
            dma((1,)),
            dma((units,)),
            dma((1,)),
            dma((1,)),
            dma((4,)),
        ],
        compiler_params=pltpu.CompilerParams(
            collective_id=0, has_side_effects=True, vmem_limit_bytes=48 << 20
        ),
        cost_estimate=pl.CostEstimate(
            flops=18 * 512 * depth * ff, bytes_accessed=12 * depth * ff, transcendentals=0
        ),
    )(*(pltpu.with_memory_space_constraint(a, pltpu.HBM) for a in (inputs, out_grad)), gate_weight, up_weight, down_weight)
    part = pl.BlockSpec((616, depth), lambda i: (i, 0))
    specs = [pl.BlockSpec(inputs.shape, lambda i: (0, 0))] + [part] * 3
    grad_input, grad_gate, grad_up, grad_down = pl.pallas_call(
        place,
        grid=(pl.cdiv(ff, 616),),
        out_shape=results,
        in_specs=specs,
        out_specs=specs,
        compiler_params=pltpu.CompilerParams(vmem_limit_bytes=10 << 20),
    )(*made)
    return grad_input, grad_gate.T, grad_up.T, grad_down


def solution(mesh):
    placed = (P("col", "row"), P("col", "row"), P("row", "col"), P("row", "col"), P("col", "row"))
    return jax.shard_map(
        on_device,
        mesh=mesh,
        in_specs=placed,
        out_specs=(P("col", "row"), P("row", "col"), P("row", "col"), P("col", "row")),
        check_vma=False,
    )
```

```python
import functools

import jax
import jax.numpy as jnp
from jax import lax
from jax.experimental import pallas as pl
from jax.experimental.pallas import tpu as pltpu
from jax.sharding import PartitionSpec as P

MESH = pl.DeviceIdType.MESH
F32, BF16 = jnp.float32, jnp.bfloat16

NEAR = [(0, 0), (0, 1), (1, 0), (1, 1), (-1, 0), (-1, 1), (2, 0), (-2, 0)]
NEAR += [(2, 1), (-2, 1), (3, 0), (3, 1), (-3, 0), (-3, 1), (4, 0), (4, 1)]
FAR = (6, 2, 4)
CHUNK = 640
UNITS = [(g, k) for g in range(2) for k in range(3)]
SUM_Y_FIRST = (True, False, True, False, True, True)
SPREAD_X_FIRST = (True, True, True, False, False, True)


def contract(left, right, left_dim, right_dim):
    return lax.dot_general(
        left,
        right,
        (((left_dim,), (right_dim,)), ((), ())),
        preferred_element_type=F32,
    )


def pointwise(gate, up, back):
    sig = jax.nn.sigmoid(gate)
    act = gate * sig
    hidden = act * up
    dgate = back * up * sig * (1.0 + gate * (1.0 - sig))
    dup = back * act
    return hidden.astype(BF16), dgate.astype(BF16), dup.astype(BF16)


def kernel(
    x_in, g_in, wg_in, wu_in, wd_in,
    gi_out, gg_out, gu_out, gd_out,
    wg, wu, wd, x_all, g_all, part, pair, terms, got, mid, cross, got_cross,
    acts, gi_acc, gi_send, gi_got, gi_lean, gg, gu, gd, gi,
    w_sem, near_send, near_recv, pair_send, pair_recv, sum_send, cross_send, sum_recv,
    act_send, act_recv, half_send, half_recv, gi_ssem, gi_rsem, lean_sem, out_sem,
):
    row, col = lax.axis_index("row"), lax.axis_index("col")
    y, h, c = row // 4, (row // 2) % 2, row % 2
    xl, z = col // 8, col % 8
    ff = wg.shape[0]

    def along(dy):
        return (y + dy) % 4

    def owner_at(dy, dh):
        return {"row": (along(dy) * 2 + (h + dh) % 2) * 2 + c, "col": col}

    def near_at(dz, dx):
        return {"row": row, "col": ((xl + dx) % 2) * 8 + (z + dz + 8) % 8}

    partner = {"row": row + 1 - 2 * c, "col": col}
    across = owner_at(0, 1)

    def remote(src, dst, send, recv, to):
        return pltpu.make_async_remote_copy(
            src_ref=src, dst_ref=dst, send_sem=send, recv_sem=recv, device_id=to, device_id_type=MESH
        )

    def settle(ref, sem):
        remote(ref, ref, sem, sem, partner).wait_recv()

    def width(k):
        return min(CHUNK, ff - k * CHUNK)

    loads = [
        pltpu.make_async_copy(src, dst, w_sem.at[i])
        for i, (src, dst) in enumerate(
            [(x_in, x_all.at[0]), (g_in, g_all.at[0]), (wg_in, wg), (wu_in, wu), (wd_in, wd)]
        )
    ]
    for load in loads:
        load.start()

    with jax.named_scope("greet"):
      barrier = pltpu.get_barrier_semaphore()
    peers = [partner, across] + [owner_at(dy, 0) for dy in (1, 3)]
    peers += [near_at(*step) for step in NEAR[1:8]]
    for peer in peers:
        pl.semaphore_signal(barrier, inc=1, device_id=peer, device_id_type=MESH)
    pl.semaphore_wait(barrier, len(peers))

    def hand(n, slot, to, at):
        ref = (x_all, g_all)[n]
        remote(ref.at[slot], ref.at[at], near_send.at[n], near_recv.at[n, at], to).start()

    seen = set()

    def arrived(n, slot):
        ref = (x_all, g_all)[n]
        if (n, slot) not in seen:
            seen.add((n, slot))
            if slot:
                remote(ref.at[slot], ref.at[slot], near_send.at[n], near_recv.at[n, slot], partner).wait_recv()
            else:
                loads[n].wait()

    def slot_of(dz, dx):
        return NEAR.index((dz, dx))

    def gather_near(n):
        arrived(n, 0)
        for slot in (6, 7, 3, 5, 2, 4, 1):
            dz, dx = NEAR[slot]
            hand(n, 0, near_at(-dz, dx), slot)

    def gather(far, dx, n):
        for way in (1, -1):
            if far == 3 and (way == 1) == bool(dx):
                continue
            slot = slot_of(-way * far, dx)
            arrived(n, slot)
            hand(n, slot, near_at(way, 0), slot_of(-way * (far + 1) if far < 3 else 4, dx))

    loaded = set()

    def weights_in(n):
        if n not in loaded:
            loaded.add(n)
            loads[n].wait()

    def landed(n, group):
        for slot in range(group * 8, group * 8 + 8):
            arrived(n, slot)

    def tokens(ref, group):
        return ref[group * 8 : group * 8 + 8].reshape(256, 512)

    def multiply(u, a, ref, weight):
        g, k = UNITS[u]
        w = width(k)
        if w < CHUNK:
            part[u, a, :, :, :, :, CHUNK - 128 :] = jnp.zeros((2, 2, 4, 16, 128), F32)
        product = contract(tokens(ref, g), weight[k * CHUNK : k * CHUNK + w, :], 1, 1)
        part[u, a, :, :, :, :, :w] = product.reshape(2, 2, 4, 16, w)
        remote(part.at[u, a, 1 - c], pair.at[u, a], pair_send.at[0], pair_recv.at[u], partner).start()

    def gate_up(u):
        landed(0, UNITS[u][0])
        weights_in(2)
        multiply(u, 0, x_all, wg)
        weights_in(3)
        multiply(u, 1, x_all, wu)

    def back(u):
        landed(1, UNITS[u][0])
        weights_in(4)
        multiply(u, 2, g_all, wd)

    def pass_to(u, src, slot, sem, dy):
        remote(src, slot, sum_send.at[u], sum_recv.at[u, sem], owner_at(dy, 0)).start()

    def own(u, a, hh, dy):
        return part[u, a, c, hh, along(dy)] + pair[u, a, hh, along(dy)]

    def sum_first(u):
        settle(pair.at[u], pair_recv.at[u])
        if SUM_Y_FIRST[u]:
            for a in range(3):
                terms[u, :, :, a] = (part[u, a, c] + pair[u, a]).astype(BF16)
            pass_to(u, terms.at[u, 0, along(2)], got.at[u, 4], 2, 1)
            pass_to(u, terms.at[u, 1, along(2)], got.at[u, 5], 3, 3)
            pass_to(u, terms.at[u, 1, along(1)], got.at[u, 1], 0, 1)
            pass_to(u, terms.at[u, 0, along(3)], got.at[u, 2], 0, 3)
        else:
            for a in range(3):
                terms[u, 1 - h, :, a] = (part[u, a, c, 1 - h] + pair[u, a, 1 - h]).astype(BF16)
            remote(terms.at[u, 1 - h], got.at[u, :4], sum_send.at[u], sum_recv.at[u, 0], across).start()

    def sum_second(u):
        if SUM_Y_FIRST[u]:
            settle(got.at[u, :4], sum_recv.at[u, 0])
            n = sum(SUM_Y_FIRST[:u])
            for a in range(3):
                total = own(u, a, 1 - h, 0)
                for i in range(2):
                    total = total + got[u, 2 * i + 1 - h, a].astype(F32)
                cross[n, a] = total
            remote(cross.at[n], got_cross.at[n], cross_send.at[0], sum_recv.at[u, 1], across).start()
        else:
            settle(got.at[u, :4], sum_recv.at[u, 0])
            for a in range(3):
                total = part[u, a, c, h] + pair[u, a, h] + got[u, :4, a].astype(F32)
                mid[u, :, a] = total.astype(BF16)
            pass_to(u, mid.at[u, along(2), 0:2], got.at[u, 6, 0:2], 2, 1)
            pass_to(u, mid.at[u, along(2), 2:3], got.at[u, 6, 2:3], 3, 3)
            pass_to(u, mid.at[u, along(1), 2:3], got.at[u, 4, 2:3], 1, 1)
            pass_to(u, mid.at[u, along(3), 0:2], got.at[u, 5, 0:2], 1, 3)

    def sum_mid(u):
        for dy in (1, 3):
            if SUM_Y_FIRST[u]:
                slot = 4 if dy == 1 else 5
                hh = 0 if dy == 1 else 1
                settle(got.at[u, slot], sum_recv.at[u, 2 if dy == 1 else 3])
                for a in range(3):
                    terms[u, hh, along(dy), a] = (own(u, a, hh, dy) + got[u, slot, a].astype(F32)).astype(BF16)
                pass_to(u, terms.at[u, hh, along(dy)], got.at[u, 0 if dy == 1 else 3], 0, dy)
            else:
                first, last = (0, 2) if dy == 1 else (2, 3)
                settle(got.at[u, 6, first:last], sum_recv.at[u, 2 if dy == 1 else 3])
                for a in range(first, last):
                    total = own(u, a, h, dy) + got[u, along(dy), a].astype(F32) + got[u, 6, a].astype(F32)
                    mid[u, along(dy), a] = total.astype(BF16)
                pass_to(
                    u, mid.at[u, along(dy), first:last], got.at[u, 4 if dy == 1 else 5, first:last], 1, dy
                )

    def block(u, dy, dh, arrays=slice(0, 3)):
        return acts.at[u, arrays, c, (h + dh) % 2, along(dy)]

    def spread(u, sem, ref, to):
        remote(ref, ref, act_send.at[u], act_recv.at[u, sem], to).start()

    def reduce(u):
        totals = []
        n = sum(SUM_Y_FIRST[:u])
        if SUM_Y_FIRST[u]:
            settle(got_cross.at[n], sum_recv.at[u, 1])
        else:
            settle(got.at[u, 4:6], sum_recv.at[u, 1])
        for a in range(3):
            total = own(u, a, h, 0)
            if SUM_Y_FIRST[u]:
                for i in range(2):
                    total = total + got[u, 2 * i + h, a].astype(F32)
                total = total + got_cross[n, a]
            else:
                total = total + got[u, y, a].astype(F32)
                for i in range(2):
                    total = total + got[u, 4 + i, a].astype(F32)
            totals.append(total)
        for a, value in enumerate(pointwise(*totals)):
            acts[u, a, c, h, y] = value
        mine = block(u, 0, 0)
        if SPREAD_X_FIRST[u]:
            spread(u, 0, mine, across)
            spread(u, 1, mine, owner_at(1, 0))
            spread(u, 3, mine, owner_at(3, 0))
        else:
            spread(u, 0, mine, owner_at(1, 0))
            spread(u, 1, mine, owner_at(3, 0))
            spread(u, 3, mine, across)

    def spread_a(u):
        settle(block(u, 0, 0), act_recv.at[u, 0])
        if SPREAD_X_FIRST[u]:
            spread(u, 3, block(u, 0, 1), owner_at(1, 0))
            spread(u, 2, block(u, 0, 1), owner_at(3, 0))
        else:
            spread(u, 2, block(u, 3, 0, slice(0, 2)), owner_at(1, 0))
            spread(u, 3, block(u, 3, 0), across)

    def spread_b(u):
        settle(block(u, 0, 0), act_recv.at[u, 1])
        if SPREAD_X_FIRST[u]:
            spread(u, 3, block(u, 3, 0), owner_at(1, 0))
        else:
            spread(u, 2, block(u, 1, 0, slice(2, 3)), owner_at(3, 0))
            spread(u, 3, block(u, 1, 0), across)

    def spread_c(u):
        settle(block(u, 0, 0), act_recv.at[u, 2])
        if SPREAD_X_FIRST[u]:
            spread(u, 3, block(u, 1, 1), owner_at(3, 0))
        else:
            spread(u, 3, block(u, 2, 0), across)

    def spread_last(u):
        settle(got.at[u, :4], act_recv.at[u, 3])
        half = acts.at[u, :, c]
        remote(half, half, half_send.at[0], half_recv.at[u], partner).start()

    def act(u, a):
        return acts[u, a].reshape(256, CHUNK)[:, : width(UNITS[u][1])]

    summed = [0, 0]

    def input_grad(u):
        g, k = UNITS[u]
        rows = slice(k * CHUNK, k * CHUNK + width(k))
        settle(acts.at[u, :, 1 - c], half_recv.at[u])
        term = contract(act(u, 1), wg[rows, :], 1, 0) + contract(act(u, 2), wu[rows, :], 1, 0)
        if summed[g] > 0:
            term = term + gi_acc[g]
        gi_acc[g] = term
        summed[g] += 1
        if summed[g] == 3:
            gi_send[g] = term.astype(BF16).reshape(8, 32, 512)
            if g == 1:
                for j, b in enumerate(FAR):
                    remote(
                        gi_send.at[1, b + 1], gi_lean.at[j], gi_ssem.at[0], lean_sem.at[j], near_at(0, 1)
                    ).start()
            for b in reversed(range(1, 8)) if g == 0 else range(2):
                give(g, b)

    def give(g, b):
        i = g * 8 + b
        remote(gi_send.at[g, b], gi_got.at[i], gi_ssem.at[0], gi_rsem.at[0], near_at(*NEAR[i])).start()

    def gi_pass(j):
        b = FAR[j]
        settle(gi_lean.at[j], lean_sem.at[j])
        gi_send[1, b] = (gi_acc[1, 32 * b : 32 * b + 32] + gi_lean[j].astype(F32)).astype(BF16)
        give(1, b)

    def weight_grads(k):
        rows = slice(k * CHUNK, k * CHUNK + width(k))
        for a, ref, out in ((1, x_all, gg), (2, x_all, gu), (0, g_all, gd)):
            total = contract(act(k, a), tokens(ref, 0), 0, 0) + contract(act(k + 3, a), tokens(ref, 1), 0, 0)
            out[rows, :] = total.astype(BF16)

    plan = [
        (gather_near, 0), (gather_near, 1),
        (gather, 1, 1, 0), (gate_up, 2), (gather, 2, 0, 0), (gate_up, 1),
        (gather, 1, 1, 1), (back, 2), (gather, 2, 0, 1), (back, 1),
        (gather, 2, 1, 0), (gather, 3, 0, 0), (gate_up, 0), (back, 0),
        (gather, 2, 1, 1), (gather, 3, 0, 1), (sum_first, 2), (sum_first, 1),
        (gather, 3, 1, 0), (gather, 3, 1, 1), (sum_first, 0), (sum_mid, 2),
        (gate_up, 4), (gate_up, 3), (back, 4), (back, 3),
        (sum_mid, 0), (gate_up, 5), (sum_second, 2), (sum_first, 4),
        (sum_second, 1), (sum_first, 3), (back, 5), (sum_second, 0),
        (sum_first, 5), (sum_mid, 4), (reduce, 2), (sum_mid, 1),
        (sum_mid, 5), (sum_second, 4), (sum_second, 3), (reduce, 1),
        (reduce, 0), (sum_second, 5), (spread_a, 2), (sum_mid, 3),
        (spread_b, 2), (reduce, 4), (spread_a, 1), (spread_b, 1),
        (spread_c, 2), (reduce, 3), (spread_a, 0), (spread_b, 0),
        (spread_a, 4), (spread_b, 4), (reduce, 5), (spread_c, 1),
        (spread_last, 2), (spread_a, 3), (spread_b, 3), (input_grad, 2),
        (spread_c, 0), (spread_c, 4), (spread_a, 5), (spread_b, 5),
        (spread_last, 1), (spread_c, 3), (spread_last, 0), (input_grad, 1),
        (spread_c, 5), (spread_last, 4), (input_grad, 0), (spread_last, 3),
        (input_grad, 4), (spread_last, 5), (weight_grads, 1), (input_grad, 3),
        (input_grad, 5), (weight_grads, 2), (weight_grads, 0), (gi_pass, 0),
        (gi_pass, 1), (gi_pass, 2),
    ]
    for stage, *at in plan:
        stage(*at)
    outs = [
        pltpu.make_async_copy(src, dst, out_sem.at[i])
        for i, (src, dst) in enumerate([(gg, gg_out), (gu, gu_out), (gd, gd_out), (gi, gi_out)])
    ]
    for out in outs[:3]:
        out.start()
    settle(gi_got.at[:12], gi_rsem.at[0])
    total = gi_acc[0, :32]
    for i in [*range(1, 10), *(8 + b for b in FAR)]:
        total = total + gi_got[i].astype(F32)
    gi[...] = total.astype(BF16)
    outs[3].start()
    settle(x_all.at[1:16], near_send.at[0])
    settle(g_all.at[1:16], near_send.at[1])
    settle(pair, pair_send.at[0])
    for u in range(len(UNITS)):
        settle(got.at[u, : 6 if SUM_Y_FIRST[u] else 7], sum_send.at[u])
        settle(got.at[u], act_send.at[u])
    settle(cross, cross_send.at[0])
    settle(terms, half_send.at[0])
    settle(gi_got.at[1:16], gi_ssem.at[0])
    for out in outs:
        out.wait()


def place(*refs):
    for source, result in zip(refs[:4], refs[4:]):
        result[...] = source[...]


def on_device(inputs, out_grad, gate_weight, up_weight, down_weight):
    rows, depth = inputs.shape
    gate_weight, up_weight = gate_weight.T, up_weight.T
    ff = gate_weight.shape[0]
    units = len(UNITS)
    dma = pltpu.SemaphoreType.DMA
    vmem = pltpu.VMEM
    weight = jax.ShapeDtypeStruct((ff, depth), BF16)
    results = (jax.ShapeDtypeStruct(inputs.shape, BF16), weight, weight, weight)
    anywhere = pl.BlockSpec(memory_space=pl.ANY)
    made = pl.pallas_call(
        kernel,
        out_shape=results,
        in_specs=[anywhere] * 5,
        out_specs=[anywhere] * 4,
        scratch_shapes=[
            vmem((ff, depth), BF16),
            vmem((ff, depth), BF16),
            vmem((ff, depth), BF16),
            vmem((16, rows, depth), BF16),
            vmem((16, rows, depth), BF16),
            vmem((units, 3, 2, 2, 4, 16, CHUNK), F32),
            vmem((units, 3, 2, 4, 16, CHUNK), F32),
            vmem((units, 2, 4, 3, 16, CHUNK), BF16),
            vmem((units, 7, 3, 16, CHUNK), BF16),
            vmem((units, 4, 3, 16, CHUNK), BF16),
            vmem((sum(SUM_Y_FIRST), 3, 16, CHUNK), F32),
            vmem((sum(SUM_Y_FIRST), 3, 16, CHUNK), F32),
            vmem((units, 3, 2, 2, 4, 16, CHUNK), BF16),
            vmem((2, 256, depth), F32),
            vmem((2, 8, rows, depth), BF16),
            vmem((16, rows, depth), BF16),
            vmem((3, rows, depth), BF16),
            vmem((ff, depth), BF16),
            vmem((ff, depth), BF16),
            vmem((ff, depth), BF16),
            vmem(inputs.shape, BF16),
            dma((5,)),
            dma((2,)),
            dma((2, 16)),
            dma((1,)),
            dma((units,)),
            dma((units,)),
            dma((1,)),
            dma((units, 4)),
            dma((units,)),
            dma((units, 4)),
            dma((1,)),
            dma((units,)),
            dma((1,)),
            dma((1,)),
            dma((3,)),
            dma((4,)),
        ],
        compiler_params=pltpu.CompilerParams(
            collective_id=0, has_side_effects=True, vmem_limit_bytes=48 << 20
        ),
        cost_estimate=pl.CostEstimate(
            flops=18 * 512 * depth * ff, bytes_accessed=12 * depth * ff, transcendentals=0
        ),
    )(*(pltpu.with_memory_space_constraint(a, pltpu.HBM) for a in (inputs, out_grad)), gate_weight, up_weight, down_weight)
    part = pl.BlockSpec((616, depth), lambda i: (i, 0))
    specs = [pl.BlockSpec(inputs.shape, lambda i: (0, 0))] + [part] * 3
    grad_input, grad_gate, grad_up, grad_down = pl.pallas_call(
        place,
        grid=(pl.cdiv(ff, 616),),
        out_shape=results,
        in_specs=specs,
        out_specs=specs,
        compiler_params=pltpu.CompilerParams(vmem_limit_bytes=10 << 20),
    )(*made)
    return grad_input, grad_gate.T, grad_up.T, grad_down


def solution(mesh):
    placed = (P("col", "row"), P("col", "row"), P("row", "col"), P("row", "col"), P("col", "row"))
    return jax.shard_map(
        on_device,
        mesh=mesh,
        in_specs=placed,
        out_specs=(P("col", "row"), P("row", "col"), P("row", "col"), P("col", "row")),
        check_vma=False,
    )
```

```python
import functools

import jax
import jax.numpy as jnp
from jax import lax
from jax.experimental import pallas as pl
from jax.experimental.pallas import tpu as pltpu
from jax.sharding import PartitionSpec as P

MESH = pl.DeviceIdType.MESH
F32, BF16 = jnp.float32, jnp.bfloat16

NEAR = [(0, 0), (0, 1), (1, 0), (1, 1), (-1, 0), (-1, 1), (2, 0), (-2, 0)]
NEAR += [(2, 1), (-2, 1), (3, 0), (3, 1), (-3, 0), (-3, 1), (4, 0), (4, 1)]
FAR = (6, 2, 4)
CHUNK = 640
UNITS = [(g, k) for g in range(2) for k in range(3)]
SUM_Y_FIRST = (False, True, True, True, False, True)
SPREAD_X_FIRST = (True, True, False, False, True, True)


def contract(left, right, left_dim, right_dim):
    return lax.dot_general(
        left,
        right,
        (((left_dim,), (right_dim,)), ((), ())),
        preferred_element_type=F32,
    )


def pointwise(gate, up, back):
    sig = jax.nn.sigmoid(gate)
    act = gate * sig
    hidden = act * up
    dgate = back * up * sig * (1.0 + gate * (1.0 - sig))
    dup = back * act
    return hidden.astype(BF16), dgate.astype(BF16), dup.astype(BF16)


def kernel(
    x_in, g_in, wg_in, wu_in, wd_in,
    gi_out, gg_out, gu_out, gd_out,
    wg, wu, wd, x_all, g_all, part, pair, terms, got, mid, cross, got_cross,
    acts, gi_acc, gi_send, gi_got, gi_lean, gg, gu, gd, gi,
    w_sem, near_send, near_recv, pair_send, pair_recv, sum_send, cross_send, sum_recv,
    act_send, act_recv, half_send, half_recv, gi_ssem, gi_rsem, lean_sem, out_sem,
):
    row, col = lax.axis_index("row"), lax.axis_index("col")
    y, h, c = row // 4, (row // 2) % 2, row % 2
    xl, z = col // 8, col % 8
    ff = wg.shape[0]

    def along(dy):
        return (y + dy) % 4

    def owner_at(dy, dh):
        return {"row": (along(dy) * 2 + (h + dh) % 2) * 2 + c, "col": col}

    def near_at(dz, dx):
        return {"row": row, "col": ((xl + dx) % 2) * 8 + (z + dz + 8) % 8}

    partner = {"row": row + 1 - 2 * c, "col": col}
    across = owner_at(0, 1)

    def remote(src, dst, send, recv, to):
        return pltpu.make_async_remote_copy(
            src_ref=src, dst_ref=dst, send_sem=send, recv_sem=recv, device_id=to, device_id_type=MESH
        )

    def settle(ref, sem):
        remote(ref, ref, sem, sem, partner).wait_recv()

    def width(k):
        return min(CHUNK, ff - k * CHUNK)

    loads = [
        pltpu.make_async_copy(src, dst, w_sem.at[i])
        for i, (src, dst) in enumerate(
            [(x_in, x_all.at[0]), (g_in, g_all.at[0]), (wg_in, wg), (wu_in, wu), (wd_in, wd)]
        )
    ]
    for load in loads:
        load.start()

    with jax.named_scope("greet"):
      barrier = pltpu.get_barrier_semaphore()
    peers = [partner, across] + [owner_at(dy, 0) for dy in (1, 3)]
    peers += [near_at(*step) for step in NEAR[1:8]]
    for peer in peers:
        pl.semaphore_signal(barrier, inc=1, device_id=peer, device_id_type=MESH)
    pl.semaphore_wait(barrier, len(peers))

    def hand(n, slot, to, at):
        ref = (x_all, g_all)[n]
        remote(ref.at[slot], ref.at[at], near_send.at[n], near_recv.at[n, at], to).start()

    seen = set()

    def arrived(n, slot):
        ref = (x_all, g_all)[n]
        if (n, slot) not in seen:
            seen.add((n, slot))
            if slot:
                remote(ref.at[slot], ref.at[slot], near_send.at[n], near_recv.at[n, slot], partner).wait_recv()
            else:
                loads[n].wait()

    def slot_of(dz, dx):
        return NEAR.index((dz, dx))

    def gather_near(n):
        arrived(n, 0)
        for slot in (6, 7, 3, 5, 2, 4, 1):
            dz, dx = NEAR[slot]
            hand(n, 0, near_at(-dz, dx), slot)

    def gather(far, dx, n):
        for way in (1, -1):
            if far == 3 and (way == 1) == bool(dx):
                continue
            slot = slot_of(-way * far, dx)
            arrived(n, slot)
            hand(n, slot, near_at(way, 0), slot_of(-way * (far + 1) if far < 3 else 4, dx))

    loaded = set()

    def weights_in(n):
        if n not in loaded:
            loaded.add(n)
            loads[n].wait()

    def landed(n, group):
        for slot in range(group * 8, group * 8 + 8):
            arrived(n, slot)

    def tokens(ref, group):
        return ref[group * 8 : group * 8 + 8].reshape(256, 512)

    def multiply(u, a, ref, weight):
        g, k = UNITS[u]
        w = width(k)
        if w < CHUNK:
            part[u, a, :, :, :, :, CHUNK - 128 :] = jnp.zeros((2, 2, 4, 16, 128), F32)
        product = contract(tokens(ref, g), weight[k * CHUNK : k * CHUNK + w, :], 1, 1)
        part[u, a, :, :, :, :, :w] = product.reshape(2, 2, 4, 16, w)
        remote(part.at[u, a, 1 - c], pair.at[u, a], pair_send.at[0], pair_recv.at[u], partner).start()

    def gate_up(u):
        landed(0, UNITS[u][0])
        weights_in(2)
        multiply(u, 0, x_all, wg)
        weights_in(3)
        multiply(u, 1, x_all, wu)

    def back(u):
        landed(1, UNITS[u][0])
        weights_in(4)
        multiply(u, 2, g_all, wd)

    def pass_to(u, src, slot, sem, dy):
        remote(src, slot, sum_send.at[u], sum_recv.at[u, sem], owner_at(dy, 0)).start()

    def own(u, a, hh, dy):
        return part[u, a, c, hh, along(dy)] + pair[u, a, hh, along(dy)]

    def sum_first(u):
        settle(pair.at[u], pair_recv.at[u])
        if SUM_Y_FIRST[u]:
            for a in range(3):
                terms[u, :, :, a] = (part[u, a, c] + pair[u, a]).astype(BF16)
            pass_to(u, terms.at[u, 0, along(2)], got.at[u, 4], 2, 1)
            pass_to(u, terms.at[u, 1, along(2)], got.at[u, 5], 3, 3)
            pass_to(u, terms.at[u, 1, along(1)], got.at[u, 1], 0, 1)
            pass_to(u, terms.at[u, 0, along(3)], got.at[u, 2], 0, 3)
        else:
            for a in range(3):
                terms[u, 1 - h, :, a] = (part[u, a, c, 1 - h] + pair[u, a, 1 - h]).astype(BF16)
            remote(terms.at[u, 1 - h], got.at[u, :4], sum_send.at[u], sum_recv.at[u, 0], across).start()

    def sum_second(u):
        if SUM_Y_FIRST[u]:
            settle(got.at[u, :4], sum_recv.at[u, 0])
            n = sum(SUM_Y_FIRST[:u])
            for a in range(3):
                total = own(u, a, 1 - h, 0)
                for i in range(2):
                    total = total + got[u, 2 * i + 1 - h, a].astype(F32)
                cross[n, a] = total
            remote(cross.at[n], got_cross.at[n], cross_send.at[0], sum_recv.at[u, 1], across).start()
        else:
            settle(got.at[u, :4], sum_recv.at[u, 0])
            for a in range(3):
                total = part[u, a, c, h] + pair[u, a, h] + got[u, :4, a].astype(F32)
                mid[u, :, a] = total.astype(BF16)
            pass_to(u, mid.at[u, along(2), 0:2], got.at[u, 6, 0:2], 2, 1)
            pass_to(u, mid.at[u, along(2), 2:3], got.at[u, 6, 2:3], 3, 3)
            pass_to(u, mid.at[u, along(1), 2:3], got.at[u, 4, 2:3], 1, 1)
            pass_to(u, mid.at[u, along(3), 0:2], got.at[u, 5, 0:2], 1, 3)

    def sum_mid(u):
        for dy in (1, 3):
            if SUM_Y_FIRST[u]:
                slot = 4 if dy == 1 else 5
                hh = 0 if dy == 1 else 1
                settle(got.at[u, slot], sum_recv.at[u, 2 if dy == 1 else 3])
                for a in range(3):
                    terms[u, hh, along(dy), a] = (own(u, a, hh, dy) + got[u, slot, a].astype(F32)).astype(BF16)
                pass_to(u, terms.at[u, hh, along(dy)], got.at[u, 0 if dy == 1 else 3], 0, dy)
            else:
                first, last = (0, 2) if dy == 1 else (2, 3)
                settle(got.at[u, 6, first:last], sum_recv.at[u, 2 if dy == 1 else 3])
                for a in range(first, last):
                    total = own(u, a, h, dy) + got[u, along(dy), a].astype(F32) + got[u, 6, a].astype(F32)
                    mid[u, along(dy), a] = total.astype(BF16)
                pass_to(
                    u, mid.at[u, along(dy), first:last], got.at[u, 4 if dy == 1 else 5, first:last], 1, dy
                )

    def block(u, dy, dh, arrays=slice(0, 3)):
        return acts.at[u, arrays, c, (h + dh) % 2, along(dy)]

    def spread(u, sem, ref, to):
        remote(ref, ref, act_send.at[u], act_recv.at[u, sem], to).start()

    def reduce(u):
        totals = []
        n = sum(SUM_Y_FIRST[:u])
        if SUM_Y_FIRST[u]:
            settle(got_cross.at[n], sum_recv.at[u, 1])
        else:
            settle(got.at[u, 4:6], sum_recv.at[u, 1])
        for a in range(3):
            total = own(u, a, h, 0)
            if SUM_Y_FIRST[u]:
                for i in range(2):
                    total = total + got[u, 2 * i + h, a].astype(F32)
                total = total + got_cross[n, a]
            else:
                total = total + got[u, y, a].astype(F32)
                for i in range(2):
                    total = total + got[u, 4 + i, a].astype(F32)
            totals.append(total)
        for a, value in enumerate(pointwise(*totals)):
            acts[u, a, c, h, y] = value
        mine = block(u, 0, 0)
        if SPREAD_X_FIRST[u]:
            spread(u, 0, mine, across)
            spread(u, 1, mine, owner_at(1, 0))
            spread(u, 3, mine, owner_at(3, 0))
        else:
            spread(u, 0, mine, owner_at(1, 0))
            spread(u, 1, mine, owner_at(3, 0))
            spread(u, 3, mine, across)

    def spread_a(u):
        settle(block(u, 0, 0), act_recv.at[u, 0])
        if SPREAD_X_FIRST[u]:
            spread(u, 3, block(u, 0, 1), owner_at(1, 0))
            spread(u, 2, block(u, 0, 1), owner_at(3, 0))
        else:
            spread(u, 2, block(u, 3, 0, slice(0, 2)), owner_at(1, 0))
            spread(u, 3, block(u, 3, 0), across)

    def spread_b(u):
        settle(block(u, 0, 0), act_recv.at[u, 1])
        if SPREAD_X_FIRST[u]:
            spread(u, 3, block(u, 3, 0), owner_at(1, 0))
        else:
            spread(u, 2, block(u, 1, 0, slice(2, 3)), owner_at(3, 0))
            spread(u, 3, block(u, 1, 0), across)

    def spread_c(u):
        settle(block(u, 0, 0), act_recv.at[u, 2])
        if SPREAD_X_FIRST[u]:
            spread(u, 3, block(u, 1, 1), owner_at(3, 0))
        else:
            spread(u, 3, block(u, 2, 0), across)

    def spread_last(u):
        settle(got.at[u, :4], act_recv.at[u, 3])
        half = acts.at[u, :, c]
        remote(half, half, half_send.at[0], half_recv.at[u], partner).start()

    def act(u, a):
        return acts[u, a].reshape(256, CHUNK)[:, : width(UNITS[u][1])]

    summed = [0, 0]

    def input_grad(u):
        g, k = UNITS[u]
        rows = slice(k * CHUNK, k * CHUNK + width(k))
        settle(acts.at[u, :, 1 - c], half_recv.at[u])
        term = contract(act(u, 1), wg[rows, :], 1, 0) + contract(act(u, 2), wu[rows, :], 1, 0)
        if summed[g] > 0:
            term = term + gi_acc[g]
        gi_acc[g] = term
        summed[g] += 1
        if summed[g] == 3:
            gi_send[g] = term.astype(BF16).reshape(8, 32, 512)
            if g == 1:
                for j, b in enumerate(FAR):
                    remote(
                        gi_send.at[1, b + 1], gi_lean.at[j], gi_ssem.at[0], lean_sem.at[j], near_at(0, 1)
                    ).start()
            for b in reversed(range(1, 8)) if g == 0 else range(2):
                give(g, b)

    def give(g, b):
        i = g * 8 + b
        remote(gi_send.at[g, b], gi_got.at[i], gi_ssem.at[0], gi_rsem.at[0], near_at(*NEAR[i])).start()

    def gi_pass(j):
        b = FAR[j]
        settle(gi_lean.at[j], lean_sem.at[j])
        gi_send[1, b] = (gi_acc[1, 32 * b : 32 * b + 32] + gi_lean[j].astype(F32)).astype(BF16)
        give(1, b)

    def weight_grads(k):
        rows = slice(k * CHUNK, k * CHUNK + width(k))
        for a, ref, out in ((1, x_all, gg), (2, x_all, gu), (0, g_all, gd)):
            total = contract(act(k, a), tokens(ref, 0), 0, 0) + contract(act(k + 3, a), tokens(ref, 1), 0, 0)
            out[rows, :] = total.astype(BF16)

    plan = [
        (gather_near, 0), (gather_near, 1),
        (gather, 1, 1, 0), (gate_up, 0), (gather, 2, 0, 0), (gate_up, 1),
        (gather, 1, 1, 1), (back, 0), (gather, 2, 0, 1), (back, 1),
        (gather, 2, 1, 0), (gather, 3, 0, 0), (sum_first, 0), (sum_first, 1),
        (gather, 2, 1, 1), (gate_up, 2), (gather, 3, 1, 0), (gather, 3, 0, 1),
        (back, 2), (gather, 3, 1, 1), (sum_mid, 1), (sum_first, 2),
        (gate_up, 3), (gate_up, 4), (back, 3), (gate_up, 5),
        (sum_second, 0), (sum_second, 1), (back, 4), (back, 5),
        (sum_first, 3), (sum_mid, 2), (sum_first, 4), (sum_mid, 0),
        (sum_first, 5), (sum_mid, 3), (reduce, 1), (sum_second, 2),
        (reduce, 0), (sum_mid, 5), (sum_second, 4), (spread_a, 1),
        (sum_second, 3), (spread_b, 1), (reduce, 2), (spread_a, 0),
        (spread_b, 0), (sum_second, 5), (sum_mid, 4), (reduce, 3),
        (spread_c, 1), (spread_a, 2), (spread_b, 2), (spread_c, 0),
        (reduce, 5), (reduce, 4), (spread_a, 3), (spread_b, 3),
        (spread_last, 1), (spread_c, 2), (spread_last, 0), (input_grad, 1),
        (spread_a, 5), (spread_b, 5), (input_grad, 0), (spread_a, 4),
        (spread_b, 4), (spread_c, 3), (spread_c, 5), (spread_last, 2),
        (spread_c, 4), (spread_last, 3), (input_grad, 2), (spread_last, 5),
        (input_grad, 3), (spread_last, 4), (weight_grads, 0), (input_grad, 5),
        (input_grad, 4), (weight_grads, 2), (weight_grads, 1), (gi_pass, 0),
        (gi_pass, 1), (gi_pass, 2),
    ]
    for stage, *at in plan:
        stage(*at)
    outs = [
        pltpu.make_async_copy(src, dst, out_sem.at[i])
        for i, (src, dst) in enumerate([(gg, gg_out), (gu, gu_out), (gd, gd_out), (gi, gi_out)])
    ]
    for out in outs[:3]:
        out.start()
    settle(gi_got.at[:12], gi_rsem.at[0])
    total = gi_acc[0, :32]
    for i in [*range(1, 10), *(8 + b for b in FAR)]:
        total = total + gi_got[i].astype(F32)
    gi[...] = total.astype(BF16)
    outs[3].start()
    settle(x_all.at[1:16], near_send.at[0])
    settle(g_all.at[1:16], near_send.at[1])
    settle(pair, pair_send.at[0])
    for u in range(len(UNITS)):
        settle(got.at[u, : 6 if SUM_Y_FIRST[u] else 7], sum_send.at[u])
        settle(got.at[u], act_send.at[u])
    settle(cross, cross_send.at[0])
    settle(terms, half_send.at[0])
    settle(gi_got.at[1:16], gi_ssem.at[0])
    for out in outs:
        out.wait()


def place(*refs):
    for source, result in zip(refs[:4], refs[4:]):
        result[...] = source[...]


def on_device(inputs, out_grad, gate_weight, up_weight, down_weight):
    rows, depth = inputs.shape
    gate_weight, up_weight = gate_weight.T, up_weight.T
    ff = gate_weight.shape[0]
    units = len(UNITS)
    dma = pltpu.SemaphoreType.DMA
    vmem = pltpu.VMEM
    weight = jax.ShapeDtypeStruct((ff, depth), BF16)
    results = (jax.ShapeDtypeStruct(inputs.shape, BF16), weight, weight, weight)
    anywhere = pl.BlockSpec(memory_space=pl.ANY)
    made = pl.pallas_call(
        kernel,
        out_shape=results,
        in_specs=[anywhere] * 5,
        out_specs=[anywhere] * 4,
        scratch_shapes=[
            vmem((ff, depth), BF16),
            vmem((ff, depth), BF16),
            vmem((ff, depth), BF16),
            vmem((16, rows, depth), BF16),
            vmem((16, rows, depth), BF16),
            vmem((units, 3, 2, 2, 4, 16, CHUNK), F32),
            vmem((units, 3, 2, 4, 16, CHUNK), F32),
            vmem((units, 2, 4, 3, 16, CHUNK), BF16),
            vmem((units, 7, 3, 16, CHUNK), BF16),
            vmem((units, 4, 3, 16, CHUNK), BF16),
            vmem((sum(SUM_Y_FIRST), 3, 16, CHUNK), F32),
            vmem((sum(SUM_Y_FIRST), 3, 16, CHUNK), F32),
            vmem((units, 3, 2, 2, 4, 16, CHUNK), BF16),
            vmem((2, 256, depth), F32),
            vmem((2, 8, rows, depth), BF16),
            vmem((16, rows, depth), BF16),
            vmem((3, rows, depth), BF16),
            vmem((ff, depth), BF16),
            vmem((ff, depth), BF16),
            vmem((ff, depth), BF16),
            vmem(inputs.shape, BF16),
            dma((5,)),
            dma((2,)),
            dma((2, 16)),
            dma((1,)),
            dma((units,)),
            dma((units,)),
            dma((1,)),
            dma((units, 4)),
            dma((units,)),
            dma((units, 4)),
            dma((1,)),
            dma((units,)),
            dma((1,)),
            dma((1,)),
            dma((3,)),
            dma((4,)),
        ],
        compiler_params=pltpu.CompilerParams(
            collective_id=0, has_side_effects=True, vmem_limit_bytes=48 << 20
        ),
        cost_estimate=pl.CostEstimate(
            flops=18 * 512 * depth * ff, bytes_accessed=12 * depth * ff, transcendentals=0
        ),
    )(*(pltpu.with_memory_space_constraint(a, pltpu.HBM) for a in (inputs, out_grad)), gate_weight, up_weight, down_weight)
    part = pl.BlockSpec((616, depth), lambda i: (i, 0))
    specs = [pl.BlockSpec(inputs.shape, lambda i: (0, 0))] + [part] * 3
    grad_input, grad_gate, grad_up, grad_down = pl.pallas_call(
        place,
        grid=(pl.cdiv(ff, 616),),
        out_shape=results,
        in_specs=specs,
        out_specs=specs,
        compiler_params=pltpu.CompilerParams(vmem_limit_bytes=10 << 20),
    )(*made)
    return grad_input, grad_gate.T, grad_up.T, grad_down


def solution(mesh):
    placed = (P("col", "row"), P("col", "row"), P("row", "col"), P("row", "col"), P("col", "row"))
    return jax.shard_map(
        on_device,
        mesh=mesh,
        in_specs=placed,
        out_specs=(P("col", "row"), P("row", "col"), P("row", "col"), P("col", "row")),
        check_vma=False,
    )
```

```python
import functools

import jax
import jax.numpy as jnp
from jax import lax
from jax.experimental import pallas as pl
from jax.experimental.pallas import tpu as pltpu
from jax.sharding import PartitionSpec as P

MESH = pl.DeviceIdType.MESH
F32, BF16 = jnp.float32, jnp.bfloat16

NEAR = [(0, 0), (0, 1), (1, 0), (1, 1), (-1, 0), (-1, 1), (2, 0), (-2, 0)]
NEAR += [(2, 1), (-2, 1), (3, 0), (3, 1), (-3, 0), (-3, 1), (4, 0), (4, 1)]
FAR = (6, 2, 4)
CHUNK = 640
UNITS = [(g, k) for g in range(2) for k in range(3)]
SUM_Y_FIRST = (False, True, True, True, False, True)
SPREAD_X_FIRST = (True, True, False, False, True, True)


def contract(left, right, left_dim, right_dim):
    return lax.dot_general(
        left,
        right,
        (((left_dim,), (right_dim,)), ((), ())),
        preferred_element_type=F32,
    )


def pointwise(gate, up, back):
    sig = jax.nn.sigmoid(gate)
    act = gate * sig
    hidden = act * up
    dgate = back * up * sig * (1.0 + gate * (1.0 - sig))
    dup = back * act
    return hidden.astype(BF16), dgate.astype(BF16), dup.astype(BF16)


def kernel(
    x_in, g_in, wg_in, wu_in, wd_in,
    gi_out, gg_out, gu_out, gd_out,
    wg, wu, wd, x_all, g_all, part, pair, terms, got, mid, cross, got_cross,
    acts, gi_acc, gi_send, gi_got, gi_lean, gg, gu, gd, gi,
    w_sem, near_send, near_recv, pair_send, pair_recv, sum_send, cross_send, sum_recv,
    act_send, act_recv, half_send, half_recv, gi_ssem, gi_rsem, lean_sem, out_sem,
):
    row, col = lax.axis_index("row"), lax.axis_index("col")
    y, h, c = row // 4, (row // 2) % 2, row % 2
    xl, z = col // 8, col % 8
    ff = wg.shape[0]

    def along(dy):
        return (y + dy) % 4

    def owner_at(dy, dh):
        return {"row": (along(dy) * 2 + (h + dh) % 2) * 2 + c, "col": col}

    def near_at(dz, dx):
        return {"row": row, "col": ((xl + dx) % 2) * 8 + (z + dz + 8) % 8}

    partner = {"row": row + 1 - 2 * c, "col": col}
    across = owner_at(0, 1)

    def remote(src, dst, send, recv, to):
        return pltpu.make_async_remote_copy(
            src_ref=src, dst_ref=dst, send_sem=send, recv_sem=recv, device_id=to, device_id_type=MESH
        )

    def settle(ref, sem):
        remote(ref, ref, sem, sem, partner).wait_recv()

    def width(k):
        return min(CHUNK, ff - k * CHUNK)

    loads = [
        pltpu.make_async_copy(src, dst, w_sem.at[i])
        for i, (src, dst) in enumerate(
            [(x_in, x_all.at[0]), (g_in, g_all.at[0]), (wg_in, wg), (wu_in, wu), (wd_in, wd)]
        )
    ]
    for load in loads:
        load.start()

    barrier = pltpu.get_barrier_semaphore()
    peers = [partner, across] + [owner_at(dy, 0) for dy in (1, 3)]
    peers += [near_at(*step) for step in NEAR[1:8]]
    for peer in peers:
        pl.semaphore_signal(barrier, inc=1, device_id=peer, device_id_type=MESH)
    pl.semaphore_wait(barrier, len(peers))

    def hand(n, slot, to, at):
        ref = (x_all, g_all)[n]
        remote(ref.at[slot], ref.at[at], near_send.at[n], near_recv.at[n, at], to).start()

    seen = set()

    def arrived(n, slot):
        ref = (x_all, g_all)[n]
        if (n, slot) not in seen:
            seen.add((n, slot))
            if slot:
                remote(ref.at[slot], ref.at[slot], near_send.at[n], near_recv.at[n, slot], partner).wait_recv()
            else:
                loads[n].wait()

    def slot_of(dz, dx):
        return NEAR.index((dz, dx))

    def gather_near(n):
        arrived(n, 0)
        for slot in (6, 7, 3, 5, 2, 4, 1):
            dz, dx = NEAR[slot]
            hand(n, 0, near_at(-dz, dx), slot)

    def gather(far, dx, n):
        for way in (1, -1):
            if far == 3 and way == -1:
                continue
            slot = slot_of(-way * far, dx)
            arrived(n, slot)
            hand(n, slot, near_at(way, 0), slot_of(-way * (far + 1) if far < 3 else 4, dx))
            if (far, dx, way) == (2, 1, -1):
                hand(n, slot, near_at(-2, 0), slot_of(4, 1))

    loaded = set()

    def weights_in(n):
        if n not in loaded:
            loaded.add(n)
            loads[n].wait()

    def landed(n, group):
        for slot in range(group * 8, group * 8 + 8):
            arrived(n, slot)

    def tokens(ref, group):
        return ref[group * 8 : group * 8 + 8].reshape(256, 512)

    def multiply(u, a, ref, weight):
        g, k = UNITS[u]
        w = width(k)
        if w < CHUNK:
            part[u, a, :, :, :, :, CHUNK - 128 :] = jnp.zeros((2, 2, 4, 16, 128), F32)
        product = contract(tokens(ref, g), weight[k * CHUNK : k * CHUNK + w, :], 1, 1)
        part[u, a, :, :, :, :, :w] = product.reshape(2, 2, 4, 16, w)
        remote(part.at[u, a, 1 - c], pair.at[u, a], pair_send.at[0], pair_recv.at[u, a // 2], partner).start()

    def gate_up(u):
        landed(0, UNITS[u][0])
        weights_in(2)
        multiply(u, 0, x_all, wg)
        weights_in(3)
        multiply(u, 1, x_all, wu)

    def back(u):
        landed(1, UNITS[u][0])
        weights_in(4)
        multiply(u, 2, g_all, wd)

    def pass_to(u, src, slot, sem, dy):
        remote(src, slot, sum_send.at[u], sum_recv.at[u, sem], owner_at(dy, 0)).start()

    def own(u, a, hh, dy):
        return part[u, a, c, hh, along(dy)] + pair[u, a, hh, along(dy)]

    def sum_first(u, start=0, stop=3):
        span = slice(start, stop)
        if start < 2:
            settle(pair.at[u, :2], pair_recv.at[u, 0])
        if stop == 3:
            settle(pair.at[u, 2], pair_recv.at[u, 1])
        if SUM_Y_FIRST[u]:
            for a in range(start, stop):
                terms[u, :, :, a] = (part[u, a, c] + pair[u, a]).astype(BF16)
            pass_to(u, terms.at[u, 0, along(2), span], got.at[u, 4, span], 2, 1)
            pass_to(u, terms.at[u, 1, along(2), span], got.at[u, 5, span], 3, 3)
            pass_to(u, terms.at[u, 1, along(1), span], got.at[u, 1, span], 0, 1)
            pass_to(u, terms.at[u, 0, along(3), span], got.at[u, 2, span], 0, 3)
        else:
            for a in range(start, stop):
                terms[u, 1 - h, :, a] = (part[u, a, c, 1 - h] + pair[u, a, 1 - h]).astype(BF16)
            remote(
                terms.at[u, 1 - h, :, span], got.at[u, :4, span], sum_send.at[u], sum_recv.at[u, 0], across
            ).start()

    def sum_second(u):
        if SUM_Y_FIRST[u]:
            settle(got.at[u, :4], sum_recv.at[u, 0])
            n = sum(SUM_Y_FIRST[:u])
            for a in range(3):
                total = own(u, a, 1 - h, 0)
                for i in range(2):
                    total = total + got[u, 2 * i + 1 - h, a].astype(F32)
                cross[n, a] = total
            remote(cross.at[n], got_cross.at[n], cross_send.at[0], sum_recv.at[u, 1], across).start()
        else:
            settle(got.at[u, :4], sum_recv.at[u, 0])
            for a in range(3):
                total = part[u, a, c, h] + pair[u, a, h] + got[u, :4, a].astype(F32)
                mid[u, :, a] = total.astype(BF16)
            pass_to(u, mid.at[u, along(2), 0:2], got.at[u, 6, 0:2], 2, 1)
            pass_to(u, mid.at[u, along(2), 2:3], got.at[u, 6, 2:3], 3, 3)
            pass_to(u, mid.at[u, along(1), 2:3], got.at[u, 4, 2:3], 1, 1)
            pass_to(u, mid.at[u, along(3), 0:2], got.at[u, 5, 0:2], 1, 3)

    def sum_mid(u):
        for dy in (1, 3):
            if SUM_Y_FIRST[u]:
                slot = 4 if dy == 1 else 5
                hh = 0 if dy == 1 else 1
                settle(got.at[u, slot], sum_recv.at[u, 2 if dy == 1 else 3])
                for a in range(3):
                    terms[u, hh, along(dy), a] = (own(u, a, hh, dy) + got[u, slot, a].astype(F32)).astype(BF16)
                pass_to(u, terms.at[u, hh, along(dy)], got.at[u, 0 if dy == 1 else 3], 0, dy)
            else:
                first, last = (0, 2) if dy == 1 else (2, 3)
                settle(got.at[u, 6, first:last], sum_recv.at[u, 2 if dy == 1 else 3])
                for a in range(first, last):
                    total = own(u, a, h, dy) + got[u, along(dy), a].astype(F32) + got[u, 6, a].astype(F32)
                    mid[u, along(dy), a] = total.astype(BF16)
                pass_to(
                    u, mid.at[u, along(dy), first:last], got.at[u, 4 if dy == 1 else 5, first:last], 1, dy
                )

    def block(u, dy, dh, arrays=slice(0, 3)):
        return acts.at[u, arrays, c, (h + dh) % 2, along(dy)]

    def spread(u, sem, ref, to):
        remote(ref, ref, act_send.at[u], act_recv.at[u, sem], to).start()

    def reduce(u):
        totals = []
        n = sum(SUM_Y_FIRST[:u])
        if SUM_Y_FIRST[u]:
            settle(got_cross.at[n], sum_recv.at[u, 1])
        else:
            settle(got.at[u, 4:6], sum_recv.at[u, 1])
        for a in range(3):
            total = own(u, a, h, 0)
            if SUM_Y_FIRST[u]:
                for i in range(2):
                    total = total + got[u, 2 * i + h, a].astype(F32)
                total = total + got_cross[n, a]
            else:
                total = total + got[u, y, a].astype(F32)
                for i in range(2):
                    total = total + got[u, 4 + i, a].astype(F32)
            totals.append(total)
        for a, value in enumerate(pointwise(*totals)):
            acts[u, a, c, h, y] = value
        mine = block(u, 0, 0)
        if SPREAD_X_FIRST[u]:
            spread(u, 0, mine, across)
            spread(u, 1, mine, owner_at(1, 0))
            spread(u, 3, mine, owner_at(3, 0))
        else:
            spread(u, 0, mine, owner_at(1, 0))
            spread(u, 1, mine, owner_at(3, 0))
            spread(u, 3, mine, across)

    def spread_a(u):
        settle(block(u, 0, 0), act_recv.at[u, 0])
        if SPREAD_X_FIRST[u]:
            spread(u, 3, block(u, 0, 1), owner_at(1, 0))
            spread(u, 2, block(u, 0, 1), owner_at(3, 0))
        else:
            spread(u, 2, block(u, 3, 0, slice(0, 2)), owner_at(1, 0))
            spread(u, 3, block(u, 3, 0), across)

    def spread_b(u):
        settle(block(u, 0, 0), act_recv.at[u, 1])
        if SPREAD_X_FIRST[u]:
            spread(u, 3, block(u, 3, 0), owner_at(1, 0))
        else:
            spread(u, 2, block(u, 1, 0, slice(2, 3)), owner_at(3, 0))
            spread(u, 3, block(u, 1, 0), across)

    def spread_c(u):
        settle(block(u, 0, 0), act_recv.at[u, 2])
        if SPREAD_X_FIRST[u]:
            spread(u, 3, block(u, 1, 1), owner_at(3, 0))
        else:
            spread(u, 3, block(u, 2, 0), across)

    def spread_last(u):
        settle(got.at[u, :4], act_recv.at[u, 3])
        half = acts.at[u, :, c]
        remote(half, half, half_send.at[0], half_recv.at[u], partner).start()

    def act(u, a):
        return acts[u, a].reshape(256, CHUNK)[:, : width(UNITS[u][1])]

    summed = [0, 0]

    def input_grad(u):
        g, k = UNITS[u]
        rows = slice(k * CHUNK, k * CHUNK + width(k))
        settle(acts.at[u, :, 1 - c], half_recv.at[u])
        term = contract(act(u, 1), wg[rows, :], 1, 0) + contract(act(u, 2), wu[rows, :], 1, 0)
        if summed[g] > 0:
            term = term + gi_acc[g]
        gi_acc[g] = term
        summed[g] += 1
        if summed[g] == 3:
            gi_send[g] = term.astype(BF16).reshape(8, 32, 512)
            if g == 1:
                for j, b in enumerate(FAR):
                    remote(
                        gi_send.at[1, b + 1], gi_lean.at[j], gi_ssem.at[0], lean_sem.at[j], near_at(0, 1)
                    ).start()
            for b in reversed(range(1, 8)) if g == 0 else range(2):
                give(g, b)

    def give(g, b):
        i = g * 8 + b
        remote(gi_send.at[g, b], gi_got.at[i], gi_ssem.at[0], gi_rsem.at[0], near_at(*NEAR[i])).start()

    def gi_pass(j):
        b = FAR[j]
        settle(gi_lean.at[j], lean_sem.at[j])
        gi_send[1, b] = (gi_acc[1, 32 * b : 32 * b + 32] + gi_lean[j].astype(F32)).astype(BF16)
        give(1, b)

    def weight_grads(k):
        rows = slice(k * CHUNK, k * CHUNK + width(k))
        for a, ref, out in ((1, x_all, gg), (2, x_all, gu), (0, g_all, gd)):
            total = contract(act(k, a), tokens(ref, 0), 0, 0) + contract(act(k + 3, a), tokens(ref, 1), 0, 0)
            out[rows, :] = total.astype(BF16)

    plan = [
        (gather_near, 0), (gather_near, 1),
        (gather, 1, 1, 0), (gate_up, 1), (gather, 2, 0, 0), (gate_up, 0),
        (gather, 1, 1, 1), (back, 1), (gather, 2, 0, 1), (sum_first, 1, 0, 2),
        (back, 0), (gather, 2, 1, 0), (sum_first, 0, 0, 2), (sum_first, 1, 2, 3),
        (gather, 3, 0, 0), (sum_first, 0, 2, 3),
        (gate_up, 2), (gather, 2, 1, 1), (gather, 3, 0, 1), (back, 2),
        (sum_mid, 1), (sum_first, 2),
        (gate_up, 3), (gate_up, 4), (back, 3), (gate_up, 5),
        (sum_second, 0), (sum_second, 1), (back, 4), (back, 5),
        (sum_first, 3), (sum_mid, 2), (sum_first, 4), (sum_mid, 0),
        (sum_first, 5), (sum_mid, 3), (reduce, 1), (sum_second, 2),
        (reduce, 0), (sum_mid, 5), (sum_second, 4), (spread_a, 1),
        (sum_second, 3), (spread_b, 1), (reduce, 2), (spread_a, 0),
        (spread_b, 0), (sum_second, 5), (sum_mid, 4), (reduce, 3),
        (spread_c, 1), (spread_a, 2), (spread_b, 2), (spread_c, 0),
        (reduce, 5), (reduce, 4), (spread_a, 3), (spread_b, 3),
        (spread_last, 1), (spread_c, 2), (spread_last, 0), (input_grad, 1),
        (spread_a, 5), (spread_b, 5), (input_grad, 0), (spread_a, 4),
        (spread_b, 4), (spread_c, 3), (spread_c, 5), (spread_last, 2),
        (spread_c, 4), (spread_last, 3), (input_grad, 2), (spread_last, 5),
        (input_grad, 3), (spread_last, 4), (weight_grads, 0), (input_grad, 5),
        (input_grad, 4), (weight_grads, 2), (weight_grads, 1), (gi_pass, 0),
        (gi_pass, 1), (gi_pass, 2),
    ]
    for stage, *at in plan:
        stage(*at)
    outs = [
        pltpu.make_async_copy(src, dst, out_sem.at[i])
        for i, (src, dst) in enumerate([(gg, gg_out), (gu, gu_out), (gd, gd_out), (gi, gi_out)])
    ]
    for out in outs[:3]:
        out.start()
    settle(gi_got.at[:12], gi_rsem.at[0])
    total = gi_acc[0, :32]
    for i in [*range(1, 10), *(8 + b for b in FAR)]:
        total = total + gi_got[i].astype(F32)
    gi[...] = total.astype(BF16)
    outs[3].start()
    settle(x_all.at[1:16], near_send.at[0])
    settle(g_all.at[1:16], near_send.at[1])
    settle(pair, pair_send.at[0])
    for u in range(len(UNITS)):
        settle(got.at[u, : 6 if SUM_Y_FIRST[u] else 7], sum_send.at[u])
        settle(got.at[u], act_send.at[u])
    settle(cross, cross_send.at[0])
    settle(terms, half_send.at[0])
    settle(gi_got.at[1:16], gi_ssem.at[0])
    for out in outs:
        out.wait()


def place(*refs):
    for source, result in zip(refs[:4], refs[4:]):
        result[...] = source[...]


def on_device(inputs, out_grad, gate_weight, up_weight, down_weight):
    rows, depth = inputs.shape
    gate_weight, up_weight = gate_weight.T, up_weight.T
    ff = gate_weight.shape[0]
    units = len(UNITS)
    dma = pltpu.SemaphoreType.DMA
    vmem = pltpu.VMEM
    weight = jax.ShapeDtypeStruct((ff, depth), BF16)
    results = (jax.ShapeDtypeStruct(inputs.shape, BF16), weight, weight, weight)
    anywhere = pl.BlockSpec(memory_space=pl.ANY)
    made = pl.pallas_call(
        kernel,
        out_shape=results,
        in_specs=[anywhere] * 5,
        out_specs=[anywhere] * 4,
        scratch_shapes=[
            vmem((ff, depth), BF16),
            vmem((ff, depth), BF16),
            vmem((ff, depth), BF16),
            vmem((16, rows, depth), BF16),
            vmem((16, rows, depth), BF16),
            vmem((units, 3, 2, 2, 4, 16, CHUNK), F32),
            vmem((units, 3, 2, 4, 16, CHUNK), F32),
            vmem((units, 2, 4, 3, 16, CHUNK), BF16),
            vmem((units, 7, 3, 16, CHUNK), BF16),
            vmem((units, 4, 3, 16, CHUNK), BF16),
            vmem((sum(SUM_Y_FIRST), 3, 16, CHUNK), F32),
            vmem((sum(SUM_Y_FIRST), 3, 16, CHUNK), F32),
            vmem((units, 3, 2, 2, 4, 16, CHUNK), BF16),
            vmem((2, 256, depth), F32),
            vmem((2, 8, rows, depth), BF16),
            vmem((16, rows, depth), BF16),
            vmem((3, rows, depth), BF16),
            vmem((ff, depth), BF16),
            vmem((ff, depth), BF16),
            vmem((ff, depth), BF16),
            vmem(inputs.shape, BF16),
            dma((5,)),
            dma((2,)),
            dma((2, 16)),
            dma((1,)),
            dma((units, 2)),
            dma((units,)),
            dma((1,)),
            dma((units, 4)),
            dma((units,)),
            dma((units, 4)),
            dma((1,)),
            dma((units,)),
            dma((1,)),
            dma((1,)),
            dma((3,)),
            dma((4,)),
        ],
        compiler_params=pltpu.CompilerParams(
            collective_id=0, has_side_effects=True, vmem_limit_bytes=48 << 20
        ),
        cost_estimate=pl.CostEstimate(
            flops=18 * 512 * depth * ff, bytes_accessed=12 * depth * ff, transcendentals=0
        ),
    )(*(pltpu.with_memory_space_constraint(a, pltpu.HBM) for a in (inputs, out_grad)), gate_weight, up_weight, down_weight)
    part = pl.BlockSpec((616, depth), lambda i: (i, 0))
    specs = [pl.BlockSpec(inputs.shape, lambda i: (0, 0))] + [part] * 3
    grad_input, grad_gate, grad_up, grad_down = pl.pallas_call(
        place,
        grid=(pl.cdiv(ff, 616),),
        out_shape=results,
        in_specs=specs,
        out_specs=specs,
        compiler_params=pltpu.CompilerParams(vmem_limit_bytes=10 << 20),
    )(*made)
    return grad_input, grad_gate.T, grad_up.T, grad_down


def solution(mesh):
    placed = (P("col", "row"), P("col", "row"), P("row", "col"), P("row", "col"), P("col", "row"))
    return jax.shard_map(
        on_device,
        mesh=mesh,
        in_specs=placed,
        out_specs=(P("col", "row"), P("row", "col"), P("row", "col"), P("col", "row")),
        check_vma=False,
    )
```

```python
import functools

import jax
import jax.numpy as jnp
from jax import lax
from jax.experimental import pallas as pl
from jax.experimental.pallas import tpu as pltpu
from jax.sharding import PartitionSpec as P

MESH = pl.DeviceIdType.MESH
F32, BF16 = jnp.float32, jnp.bfloat16

NEAR = [(0, 0), (0, 1), (1, 0), (1, 1), (-1, 0), (-1, 1), (2, 0), (-2, 0)]
NEAR += [(2, 1), (-2, 1), (3, 0), (3, 1), (-3, 0), (-3, 1), (4, 0), (4, 1)]
FAR = (6, 2, 4)
CHUNK = 640
UNITS = [(g, k) for g in range(2) for k in range(3)]
SUM_Y_FIRST = (False, True, True, True, False, True)
SPREAD_X_FIRST = (True, True, False, False, True, True)


def contract(left, right, left_dim, right_dim):
    return lax.dot_general(
        left,
        right,
        (((left_dim,), (right_dim,)), ((), ())),
        preferred_element_type=F32,
    )


def pointwise(gate, up, back):
    sig = jax.nn.sigmoid(gate)
    act = gate * sig
    hidden = act * up
    dgate = back * up * sig * (1.0 + gate * (1.0 - sig))
    dup = back * act
    return hidden.astype(BF16), dgate.astype(BF16), dup.astype(BF16)


def kernel(
    x_in, g_in, wg_in, wu_in, wd_in,
    gi_out, gg_out, gu_out, gd_out,
    wg, wu, wd, x_all, g_all, part, pair, terms, got, mid, cross, got_cross,
    acts, gi_acc, gi_send, gi_got, gi_lean, gg, gu, gd, gi,
    w_sem, near_send, near_recv, pair_send, pair_recv, sum_send, cross_send, sum_recv,
    act_send, act_recv, half_send, half_recv, gi_ssem, gi_rsem, lean_sem, out_sem,
):
    row, col = lax.axis_index("row"), lax.axis_index("col")
    y, h, c = row // 4, (row // 2) % 2, row % 2
    xl, z = col // 8, col % 8
    ff = wg.shape[0]

    def along(dy):
        return (y + dy) % 4

    def owner_at(dy, dh):
        return {"row": (along(dy) * 2 + (h + dh) % 2) * 2 + c, "col": col}

    def near_at(dz, dx):
        return {"row": row, "col": ((xl + dx) % 2) * 8 + (z + dz + 8) % 8}

    partner = {"row": row + 1 - 2 * c, "col": col}
    across = owner_at(0, 1)

    def remote(src, dst, send, recv, to):
        return pltpu.make_async_remote_copy(
            src_ref=src, dst_ref=dst, send_sem=send, recv_sem=recv, device_id=to, device_id_type=MESH
        )

    def settle(ref, sem):
        remote(ref, ref, sem, sem, partner).wait_recv()

    def width(k):
        return min(CHUNK, ff - k * CHUNK)

    loads = [
        pltpu.make_async_copy(src, dst, w_sem.at[i])
        for i, (src, dst) in enumerate(
            [(x_in, x_all.at[0]), (g_in, g_all.at[0]), (wg_in, wg), (wu_in, wu), (wd_in, wd)]
        )
    ]
    for load in loads:
        load.start()

    barrier = pltpu.get_barrier_semaphore()
    peers = [partner, across] + [owner_at(dy, 0) for dy in (1, 3)]
    peers += [near_at(*step) for step in NEAR[1:8]]
    for peer in peers:
        pl.semaphore_signal(barrier, inc=1, device_id=peer, device_id_type=MESH)
    pl.semaphore_wait(barrier, len(peers))

    def hand(n, slot, to, at):
        ref = (x_all, g_all)[n]
        remote(ref.at[slot], ref.at[at], near_send.at[n], near_recv.at[n, at], to).start()

    seen = set()

    def arrived(n, slot):
        ref = (x_all, g_all)[n]
        if (n, slot) not in seen:
            seen.add((n, slot))
            if slot:
                remote(ref.at[slot], ref.at[slot], near_send.at[n], near_recv.at[n, slot], partner).wait_recv()
            else:
                loads[n].wait()

    def slot_of(dz, dx):
        return NEAR.index((dz, dx))

    def gather_near(n):
        arrived(n, 0)
        for slot in (6, 7, 3, 5, 2, 4, 1):
            dz, dx = NEAR[slot]
            hand(n, 0, near_at(-dz, dx), slot)

    def gather(far, dx, n):
        for way in (1, -1):
            if far == 3 and way == -1:
                continue
            slot = slot_of(-way * far, dx)
            arrived(n, slot)
            hand(n, slot, near_at(way, 0), slot_of(-way * (far + 1) if far < 3 else 4, dx))
            if (far, dx, way) == (2, 1, -1):
                hand(n, slot, near_at(-2, 0), slot_of(4, 1))

    loaded = set()

    def weights_in(n):
        if n not in loaded:
            loaded.add(n)
            loads[n].wait()

    def landed(n, group):
        for slot in range(group * 8, group * 8 + 8):
            arrived(n, slot)

    def tokens(ref, group):
        return ref[group * 8 : group * 8 + 8].reshape(256, 512)

    def multiply(u, a, ref, weight):
        g, k = UNITS[u]
        w = width(k)
        if w < CHUNK:
            part[u, a, :, :, :, :, CHUNK - 128 :] = jnp.zeros((2, 2, 4, 16, 128), F32)
        product = contract(tokens(ref, g), weight[k * CHUNK : k * CHUNK + w, :], 1, 1)
        part[u, a, :, :, :, :, :w] = product.reshape(2, 2, 4, 16, w)
        remote(part.at[u, a, 1 - c], pair.at[u, a], pair_send.at[0], pair_recv.at[u, a // 2], partner).start()

    def gate_up(u):
        landed(0, UNITS[u][0])
        weights_in(2)
        multiply(u, 0, x_all, wg)
        weights_in(3)
        multiply(u, 1, x_all, wu)

    def back(u):
        landed(1, UNITS[u][0])
        weights_in(4)
        multiply(u, 2, g_all, wd)

    def pass_to(u, src, slot, sem, dy):
        remote(src, slot, sum_send.at[u], sum_recv.at[u, sem], owner_at(dy, 0)).start()

    def own(u, a, hh, dy):
        return part[u, a, c, hh, along(dy)] + pair[u, a, hh, along(dy)]

    def sum_first(u, start=0, stop=3):
        span = slice(start, stop)
        if start < 2:
            settle(pair.at[u, :2], pair_recv.at[u, 0])
        if stop == 3:
            settle(pair.at[u, 2], pair_recv.at[u, 1])
        if SUM_Y_FIRST[u]:
            for a in range(start, stop):
                terms[u, :, :, a] = (part[u, a, c] + pair[u, a]).astype(BF16)
            pass_to(u, terms.at[u, 0, along(2), span], got.at[u, 4, span], 2, 1)
            pass_to(u, terms.at[u, 1, along(2), span], got.at[u, 5, span], 3, 3)
            pass_to(u, terms.at[u, 1, along(1), span], got.at[u, 1, span], 0, 1)
            pass_to(u, terms.at[u, 0, along(3), span], got.at[u, 2, span], 0, 3)
        else:
            for a in range(start, stop):
                terms[u, 1 - h, :, a] = (part[u, a, c, 1 - h] + pair[u, a, 1 - h]).astype(BF16)
            remote(
                terms.at[u, 1 - h, :, span], got.at[u, :4, span], sum_send.at[u], sum_recv.at[u, 0], across
            ).start()

    def sum_second(u):
        if SUM_Y_FIRST[u]:
            settle(got.at[u, :4], sum_recv.at[u, 0])
            n = sum(SUM_Y_FIRST[:u])
            for a in range(3):
                total = own(u, a, 1 - h, 0)
                for i in range(2):
                    total = total + got[u, 2 * i + 1 - h, a].astype(F32)
                cross[n, a] = total
            remote(cross.at[n], got_cross.at[n], cross_send.at[0], sum_recv.at[u, 1], across).start()
        else:
            settle(got.at[u, :4], sum_recv.at[u, 0])
            for a in range(3):
                total = part[u, a, c, h] + pair[u, a, h] + got[u, :4, a].astype(F32)
                mid[u, :, a] = total.astype(BF16)
            pass_to(u, mid.at[u, along(2), 0:2], got.at[u, 6, 0:2], 2, 1)
            pass_to(u, mid.at[u, along(2), 2:3], got.at[u, 6, 2:3], 3, 3)
            pass_to(u, mid.at[u, along(1), 2:3], got.at[u, 4, 2:3], 1, 1)
            pass_to(u, mid.at[u, along(3), 0:2], got.at[u, 5, 0:2], 1, 3)

    def sum_mid(u):
        for dy in (1, 3):
            if SUM_Y_FIRST[u]:
                slot = 4 if dy == 1 else 5
                hh = 0 if dy == 1 else 1
                settle(got.at[u, slot], sum_recv.at[u, 2 if dy == 1 else 3])
                for a in range(3):
                    terms[u, hh, along(dy), a] = (own(u, a, hh, dy) + got[u, slot, a].astype(F32)).astype(BF16)
                pass_to(u, terms.at[u, hh, along(dy)], got.at[u, 0 if dy == 1 else 3], 0, dy)
            else:
                first, last = (0, 2) if dy == 1 else (2, 3)
                settle(got.at[u, 6, first:last], sum_recv.at[u, 2 if dy == 1 else 3])
                for a in range(first, last):
                    total = own(u, a, h, dy) + got[u, along(dy), a].astype(F32) + got[u, 6, a].astype(F32)
                    mid[u, along(dy), a] = total.astype(BF16)
                pass_to(
                    u, mid.at[u, along(dy), first:last], got.at[u, 4 if dy == 1 else 5, first:last], 1, dy
                )

    def block(u, dy, dh, arrays=slice(0, 3)):
        return acts.at[u, arrays, c, (h + dh) % 2, along(dy)]

    def spread(u, sem, ref, to):
        remote(ref, ref, act_send.at[u], act_recv.at[u, sem], to).start()

    def reduce(u):
        totals = []
        n = sum(SUM_Y_FIRST[:u])
        if SUM_Y_FIRST[u]:
            settle(got_cross.at[n], sum_recv.at[u, 1])
        else:
            settle(got.at[u, 4:6], sum_recv.at[u, 1])
        for a in range(3):
            total = own(u, a, h, 0)
            if SUM_Y_FIRST[u]:
                for i in range(2):
                    total = total + got[u, 2 * i + h, a].astype(F32)
                total = total + got_cross[n, a]
            else:
                total = total + got[u, y, a].astype(F32)
                for i in range(2):
                    total = total + got[u, 4 + i, a].astype(F32)
            totals.append(total)
        for a, value in enumerate(pointwise(*totals)):
            acts[u, a, c, h, y] = value
        mine = block(u, 0, 0)
        if SPREAD_X_FIRST[u]:
            spread(u, 0, mine, across)
            spread(u, 1, mine, owner_at(1, 0))
            spread(u, 3, mine, owner_at(3, 0))
        else:
            spread(u, 0, mine, owner_at(1, 0))
            spread(u, 1, mine, owner_at(3, 0))
            spread(u, 3, mine, across)

    def spread_a(u):
        settle(block(u, 0, 0), act_recv.at[u, 0])
        if SPREAD_X_FIRST[u]:
            spread(u, 3, block(u, 0, 1), owner_at(1, 0))
            spread(u, 2, block(u, 0, 1), owner_at(3, 0))
        else:
            spread(u, 2, block(u, 3, 0, slice(0, 2)), owner_at(1, 0))
            spread(u, 3, block(u, 3, 0), across)

    def spread_b(u):
        settle(block(u, 0, 0), act_recv.at[u, 1])
        if SPREAD_X_FIRST[u]:
            spread(u, 3, block(u, 3, 0), owner_at(1, 0))
        else:
            spread(u, 2, block(u, 1, 0, slice(2, 3)), owner_at(3, 0))
            spread(u, 3, block(u, 1, 0), across)

    def spread_c(u):
        settle(block(u, 0, 0), act_recv.at[u, 2])
        if SPREAD_X_FIRST[u]:
            spread(u, 3, block(u, 1, 1), owner_at(3, 0))
        else:
            spread(u, 3, block(u, 2, 0), across)

    def spread_last(u):
        settle(got.at[u, :4], act_recv.at[u, 3])
        half = acts.at[u, :, c]
        remote(half, half, half_send.at[0], half_recv.at[u], partner).start()

    def act(u, a):
        return acts[u, a].reshape(256, CHUNK)[:, : width(UNITS[u][1])]

    summed = [0, 0]

    def input_grad(u):
        g, k = UNITS[u]
        rows = slice(k * CHUNK, k * CHUNK + width(k))
        settle(acts.at[u, :, 1 - c], half_recv.at[u])
        term = contract(act(u, 1), wg[rows, :], 1, 0) + contract(act(u, 2), wu[rows, :], 1, 0)
        if summed[g] > 0:
            term = term + gi_acc[g]
        gi_acc[g] = term
        summed[g] += 1
        if summed[g] == 3:
            gi_send[g] = term.astype(BF16).reshape(8, 32, 512)
            if g == 1:
                for j, b in enumerate(FAR):
                    remote(
                        gi_send.at[1, b + 1], gi_lean.at[j], gi_ssem.at[0], lean_sem.at[j], near_at(0, 1)
                    ).start()
            for b in reversed(range(1, 8)) if g == 0 else range(2):
                give(g, b)

    def give(g, b):
        i = g * 8 + b
        remote(gi_send.at[g, b], gi_got.at[i], gi_ssem.at[0], gi_rsem.at[0], near_at(*NEAR[i])).start()

    def gi_pass(j):
        b = FAR[j]
        settle(gi_lean.at[j], lean_sem.at[j])
        gi_send[1, b] = (gi_acc[1, 32 * b : 32 * b + 32] + gi_lean[j].astype(F32)).astype(BF16)
        give(1, b)

    def weight_grads(k):
        rows = slice(k * CHUNK, k * CHUNK + width(k))
        for a, ref, out in ((1, x_all, gg), (2, x_all, gu), (0, g_all, gd)):
            total = contract(act(k, a), tokens(ref, 0), 0, 0) + contract(act(k + 3, a), tokens(ref, 1), 0, 0)
            out[rows, :] = total.astype(BF16)

    plan = [
        (gather_near, 0), (gather_near, 1),
        (gather, 1, 1, 0), (gate_up, 1), (gather, 2, 0, 0), (gate_up, 0),
        (gather, 1, 1, 1), (back, 1), (gather, 2, 0, 1), (sum_first, 1, 0, 2),
        (back, 0), (gather, 2, 1, 0), (sum_first, 0, 0, 2), (sum_first, 1, 2, 3),
        (gather, 3, 0, 0), (sum_first, 0, 2, 3),
        (gate_up, 2), (gather, 2, 1, 1), (gather, 3, 0, 1), (back, 2),
        (sum_first, 2, 0, 2), (sum_mid, 1), (sum_first, 2, 2, 3),
        (gate_up, 3), (gate_up, 4), (back, 3), (gate_up, 5),
        (sum_second, 0), (sum_second, 1), (back, 4), (back, 5),
        (sum_first, 3), (sum_mid, 2), (sum_first, 4), (sum_mid, 0),
        (sum_first, 5), (sum_mid, 3), (reduce, 1), (sum_second, 2),
        (reduce, 0), (sum_mid, 5), (sum_second, 4), (spread_a, 1),
        (sum_second, 3), (spread_b, 1), (reduce, 2), (spread_a, 0),
        (spread_b, 0), (sum_second, 5), (sum_mid, 4), (reduce, 3),
        (spread_c, 1), (spread_a, 2), (spread_b, 2), (spread_c, 0),
        (reduce, 5), (reduce, 4), (spread_a, 3), (spread_b, 3),
        (spread_last, 1), (spread_c, 2), (spread_last, 0), (input_grad, 1),
        (spread_a, 5), (spread_b, 5), (input_grad, 0), (spread_a, 4),
        (spread_b, 4), (spread_c, 3), (spread_c, 5), (spread_last, 2),
        (spread_c, 4), (spread_last, 3), (input_grad, 2), (spread_last, 5),
        (input_grad, 3), (spread_last, 4), (weight_grads, 0), (input_grad, 5),
        (input_grad, 4), (weight_grads, 2), (weight_grads, 1), (gi_pass, 0),
        (gi_pass, 1), (gi_pass, 2),
    ]
    for stage, *at in plan:
        stage(*at)
    outs = [
        pltpu.make_async_copy(src, dst, out_sem.at[i])
        for i, (src, dst) in enumerate([(gg, gg_out), (gu, gu_out), (gd, gd_out), (gi, gi_out)])
    ]
    for out in outs[:3]:
        out.start()
    settle(gi_got.at[:12], gi_rsem.at[0])
    total = gi_acc[0, :32]
    for i in [*range(1, 10), *(8 + b for b in FAR)]:
        total = total + gi_got[i].astype(F32)
    gi[...] = total.astype(BF16)
    outs[3].start()
    settle(x_all.at[1:16], near_send.at[0])
    settle(g_all.at[1:16], near_send.at[1])
    settle(pair, pair_send.at[0])
    for u in range(len(UNITS)):
        settle(got.at[u, : 6 if SUM_Y_FIRST[u] else 7], sum_send.at[u])
        settle(got.at[u], act_send.at[u])
    settle(cross, cross_send.at[0])
    settle(terms, half_send.at[0])
    settle(gi_got.at[1:16], gi_ssem.at[0])
    for out in outs:
        out.wait()


def place(*refs):
    for source, result in zip(refs[:4], refs[4:]):
        result[...] = source[...]


def on_device(inputs, out_grad, gate_weight, up_weight, down_weight):
    rows, depth = inputs.shape
    gate_weight, up_weight = gate_weight.T, up_weight.T
    ff = gate_weight.shape[0]
    units = len(UNITS)
    dma = pltpu.SemaphoreType.DMA
    vmem = pltpu.VMEM
    weight = jax.ShapeDtypeStruct((ff, depth), BF16)
    results = (jax.ShapeDtypeStruct(inputs.shape, BF16), weight, weight, weight)
    anywhere = pl.BlockSpec(memory_space=pl.ANY)
    made = pl.pallas_call(
        kernel,
        out_shape=results,
        in_specs=[anywhere] * 5,
        out_specs=[anywhere] * 4,
        scratch_shapes=[
            vmem((ff, depth), BF16),
            vmem((ff, depth), BF16),
            vmem((ff, depth), BF16),
            vmem((16, rows, depth), BF16),
            vmem((16, rows, depth), BF16),
            vmem((units, 3, 2, 2, 4, 16, CHUNK), F32),
            vmem((units, 3, 2, 4, 16, CHUNK), F32),
            vmem((units, 2, 4, 3, 16, CHUNK), BF16),
            vmem((units, 7, 3, 16, CHUNK), BF16),
            vmem((units, 4, 3, 16, CHUNK), BF16),
            vmem((sum(SUM_Y_FIRST), 3, 16, CHUNK), F32),
            vmem((sum(SUM_Y_FIRST), 3, 16, CHUNK), F32),
            vmem((units, 3, 2, 2, 4, 16, CHUNK), BF16),
            vmem((2, 256, depth), F32),
            vmem((2, 8, rows, depth), BF16),
            vmem((16, rows, depth), BF16),
            vmem((3, rows, depth), BF16),
            vmem((ff, depth), BF16),
            vmem((ff, depth), BF16),
            vmem((ff, depth), BF16),
            vmem(inputs.shape, BF16),
            dma((5,)),
            dma((2,)),
            dma((2, 16)),
            dma((1,)),
            dma((units, 2)),
            dma((units,)),
            dma((1,)),
            dma((units, 4)),
            dma((units,)),
            dma((units, 4)),
            dma((1,)),
            dma((units,)),
            dma((1,)),
            dma((1,)),
            dma((3,)),
            dma((4,)),
        ],
        compiler_params=pltpu.CompilerParams(
            collective_id=0, has_side_effects=True, vmem_limit_bytes=48 << 20
        ),
        cost_estimate=pl.CostEstimate(
            flops=18 * 512 * depth * ff, bytes_accessed=12 * depth * ff, transcendentals=0
        ),
    )(*(pltpu.with_memory_space_constraint(a, pltpu.HBM) for a in (inputs, out_grad)), gate_weight, up_weight, down_weight)
    part = pl.BlockSpec((616, depth), lambda i: (i, 0))
    specs = [pl.BlockSpec(inputs.shape, lambda i: (0, 0))] + [part] * 3
    grad_input, grad_gate, grad_up, grad_down = pl.pallas_call(
        place,
        grid=(pl.cdiv(ff, 616),),
        out_shape=results,
        in_specs=specs,
        out_specs=specs,
        compiler_params=pltpu.CompilerParams(vmem_limit_bytes=10 << 20),
    )(*made)
    return grad_input, grad_gate.T, grad_up.T, grad_down


def solution(mesh):
    placed = (P("col", "row"), P("col", "row"), P("row", "col"), P("row", "col"), P("col", "row"))
    return jax.shard_map(
        on_device,
        mesh=mesh,
        in_specs=placed,
        out_specs=(P("col", "row"), P("row", "col"), P("row", "col"), P("col", "row")),
        check_vma=False,
    )
```
